512 devices in a mesh: rows: 32 (over z, core), bal: 16 (over x, y).
Axes of the slice: x: 4, y: 4, z: 16, core: 2. Of those that a mesh axis runs over, the one named last changes fastest.
Arguments:
- rhs: float32 [1024, 256], P(('rows', 'bal'))
- self_term: float32 [1024, 256], P(('rows', 'bal')), may hold values from 2.5 to 6
- near_dense_blocks: bfloat16 [4096, 256, 256], P(('rows', 'bal')), may hold values from -0.125 to 0.125
- near_row: int32 [4096], P(('rows', 'bal')), may hold values from 0 to 1023, as said below
- near_column_cluster: int32 [4096], P(('rows', 'bal')), may hold values from 0 to 1023, as said below
- far_left: bfloat16 [3072, 32, 256], P(('rows', 'bal')), may hold values from -0.4375 to 0.4375
- far_right: bfloat16 [3072, 32, 256], P(('rows', 'bal')), may hold values from -0.375 to 0.375
- far_row: int32 [3072], P(('rows', 'bal')), may hold values from 0 to 1023, as said below
- far_col: int32 [3072], P(('rows', 'bal')), may hold values from 0 to 1023
- far_rank: int32 [3072], P(('rows', 'bal')), may hold values from 8 to 32
Outputs:
- solution: float32 [1024, 256], P(('rows', 'bal'))
- next_basis: float32 [1024, 256], P(('rows', 'bal'))
The draws below stay inside these ranges and needn't reach their ends.
Inputs may be any that keep to these rules, and one draw needn't show every extreme that they name: `near_row`: the row cluster of every near block lies among the 32 row clusters of the index of rows that holds the block. `near_column_cluster`: the column cluster of a near block is at most 3 clusters away from its row cluster, cyclically. `far_row`: the row cluster of every far block lies among the 32 row clusters of the index of rows that holds the block.
All inputs are finite; a program needn't handle non-finite values.
Results may differ from the reference program's by a relative error of at most 0.0163.
Values may be sent and summed in bfloat16 or wider, within the bound.
A program may use at most 64 MiB of HBM per device.

```python
import math
import jax
import jax.numpy as jnp
from jax import lax

CLUSTER_UNKNOWNS = 256
RANK = 32
DEVICE_CLUSTERS = 2
NEAR_TASK_COUNT = 8
FSLOT = 6
CG = 32
C = 1024
NEAR_COUNT = 4096
FAR = 3072
N_BAL = 16


def near_pattern(key):
    task_places = jnp.arange(NEAR_COUNT, dtype=jnp.int32)
    task_group = task_places // (NEAR_TASK_COUNT * N_BAL)
    local = jax.random.randint(jax.random.fold_in(key, 11), (NEAR_COUNT,), 0, CG, dtype=jnp.int32)
    row = task_group * CG + local
    offset = jax.random.randint(jax.random.fold_in(key, 12), (NEAR_COUNT,), -3, 4, dtype=jnp.int32)
    col = (row + offset + C) % C
    return (row, col)


def draw_near_row(key, part):
    row, col = near_pattern(key)
    return row


def draw_near_column_cluster(key, part):
    row, col = near_pattern(key)
    return col


def draw_far_row(key, part):
    key = jax.random.fold_in(key, 21)
    task_places = jnp.arange(FAR, dtype=jnp.int32)
    task_group = task_places // (FSLOT * N_BAL)
    local = jax.random.randint(key, (FAR,), 0, CG, dtype=jnp.int32)
    return task_group * CG + local


def draw_far_col(key, part):
    key = jax.random.fold_in(key, 22)
    return jax.random.randint(key, (FAR,), 0, C, dtype=jnp.int32)


def draw_far_rank(key, part):
    key = jax.random.fold_in(key, 23)
    ranks = jax.random.randint(key, (FAR,), RANK // 4, RANK + 1, dtype=jnp.int32)
    place = jnp.arange(FAR, dtype=jnp.int32)
    ranks = jnp.where(place == 0, RANK, ranks)
    return jnp.where(place == 1, RANK // 4, ranks)


def draw_rhs(key, part):
    key = jax.random.fold_in(key, 31)
    ramp = 1.0 + 2.0 * jnp.arange(C, dtype=jnp.float32)[:, None] / max(C - 1, 1)
    rough = jax.random.normal(jax.random.fold_in(key, 3), (C, CLUSTER_UNKNOWNS), jnp.float32)
    return jnp.clip(rough, -6.0, 6.0) * ramp


def steps_of(key, shape, cuts, least, largest):
    def one(dim, shards_of):
        steps = jax.random.uniform(jax.random.fold_in(jax.random.fold_in(key, 6), dim), (shards_of,), jnp.float32, least / len(cuts), largest / len(cuts))
        return jnp.repeat(jnp.exp(steps), shape[dim] // shards_of).reshape((-1,) + (1,) * (len(shape) - dim - 1))

    factor_of = one(*cuts[0])
    for cut in cuts[1:]:
        factor_of = factor_of * one(*cut)
    return factor_of


def normal_values(rng, extent, deviation, bound, split=(), kind=jnp.bfloat16):
    values = jax.random.normal(rng, extent, jnp.float32) * deviation
    if len(split) > 0:
        values = steps_of(rng, extent, split, -0.22, 0.18) * values
    return jnp.clip(values, min=-bound, max=bound).astype(kind)


def setup_inputs(seed: int = 0) -> dict:
    key_list = jax.random.split(jax.random.key(seed), 11)
    return {
        "rhs": draw_rhs(jax.random.fold_in(key_list[10], 71), 0),
        "self_term": jnp.clip(jnp.exp(math.log(6.0) - 0.87546874 * jax.random.uniform(key_list[1], (C, CLUSTER_UNKNOWNS), jnp.float32) ** steps_of(key_list[1], (C, CLUSTER_UNKNOWNS), ((0, 512),), -0.2, 0.2)), 2.5, 6.0),
        "near_dense_blocks": normal_values(key_list[2], (NEAR_COUNT, CLUSTER_UNKNOWNS, CLUSTER_UNKNOWNS), (2 * CLUSTER_UNKNOWNS * NEAR_TASK_COUNT // DEVICE_CLUSTERS) ** -0.5, 0.125, ((0, 512),)),
        "near_row": draw_near_row(jax.random.fold_in(key_list[10], 71), 0),
        "near_column_cluster": draw_near_column_cluster(jax.random.fold_in(key_list[10], 71), 0),
        "far_left": normal_values(key_list[5], (FAR, RANK, CLUSTER_UNKNOWNS), (2 * RANK * FSLOT // DEVICE_CLUSTERS) ** -0.5, 0.4375, ((0, 512),)),
        "far_right": normal_values(key_list[6], (FAR, RANK, CLUSTER_UNKNOWNS), CLUSTER_UNKNOWNS ** -0.5, 0.375, ((0, 512),)),
        "far_row": draw_far_row(jax.random.fold_in(key_list[10], 71), 0),
        "far_col": draw_far_col(jax.random.fold_in(key_list[10], 71), 0),
        "far_rank": draw_far_rank(jax.random.fold_in(key_list[10], 71), 0),
    }


def apply_operator(vec, self_term, near_dense_blocks, near_row, near_column_cluster, far_left, far_right, far_row, far_col, far_rank):
    source = vec.astype(jnp.bfloat16)

    def near_portion(args):
        blocks, cols = args
        picked = source[cols].astype(jnp.float32)
        return jnp.einsum('kij,kj->ki', blocks.astype(jnp.float32), picked)
    near_contributions = lax.map(near_portion, (near_dense_blocks.reshape(-1, NEAR_TASK_COUNT, CLUSTER_UNKNOWNS, CLUSTER_UNKNOWNS), near_column_cluster.reshape(-1, NEAR_TASK_COUNT).astype(jnp.int32)))
    near_sum = jax.ops.segment_sum(near_contributions.reshape(-1, CLUSTER_UNKNOWNS), near_row, num_segments=C)

    def far_part(args):
        left, right, cols, ranks = args
        picked = source[cols].astype(jnp.float32)
        coeff = jnp.einsum('krj,kj->kr', right.astype(jnp.float32), picked)
        keep = jnp.arange(RANK, dtype=jnp.int32)[None, :] < ranks[:, None]
        coeff = jnp.where(keep, coeff, 0.0).astype(jnp.bfloat16)
        return jnp.einsum('krj,kr->kj', left.astype(jnp.float32), coeff.astype(jnp.float32))
    far_terms = lax.map(far_part, (far_left.reshape(-1, FSLOT, RANK, CLUSTER_UNKNOWNS), far_right.reshape(-1, FSLOT, RANK, CLUSTER_UNKNOWNS), far_col.reshape(-1, FSLOT), far_rank.reshape(-1, FSLOT)))
    far_sum = jax.ops.segment_sum(far_terms.reshape(-1, CLUSTER_UNKNOWNS), far_row, num_segments=C)
    return self_term * vec + near_sum + far_sum

def reference(rhs, self_term, near_dense_blocks, near_row, near_column_cluster, far_left, far_right, far_row, far_col, far_rank):

    def operate(vec):
        return apply_operator(vec, self_term, near_dense_blocks, near_row, near_column_cluster, far_left, far_right, far_row, far_col, far_rank)
    beta = jnp.sqrt(jnp.sum(rhs * rhs))
    first = rhs / beta
    image = operate(first)
    h11 = jnp.sum(first * image)
    remain = image - h11 * first
    h21 = jnp.sqrt(jnp.sum(remain * remain) + 1e-06)
    second = remain / h21
    image = operate(second)
    h12 = jnp.sum(first * image)
    h22 = jnp.sum(second * image)
    remain = image - h12 * first - h22 * second
    h32 = jnp.sqrt(jnp.sum(remain * remain) + 1e-06)
    next_basis = remain / h32
    radius = jnp.sqrt(h11 * h11 + h21 * h21)
    cosine = h11 / radius
    sine = h21 / radius
    upper = cosine * h12 + sine * h22
    lower = cosine * h22 - sine * h12
    radius_two = jnp.sqrt(lower * lower + h32 * h32)
    coef_two = -(lower / radius_two) * sine * beta / radius_two
    coef_one = (cosine * beta - upper * coef_two) / radius
    solution = coef_one * first + coef_two * second
    return (solution, next_basis)
```

```python
import jax
import jax.numpy as jnp
from jax import lax
from jax.experimental import pallas as pl
from jax.experimental.pallas import tpu as pltpu
from jax.sharding import PartitionSpec as P

MESH = pl.DeviceIdType.MESH
F32 = jnp.float32
BF16 = jnp.bfloat16
NEAR, FARS, RANK = 8, 6, 32

RING_HOPS = (0, 1, 2, 1)
PLANE = sorted(range(1, 16), key=lambda j: -(RING_HOPS[j // 4] + RING_HOPS[j % 4]))
ALONG = sorted(range(1, 16), key=lambda i: -min(i, 16 - i))
SLOT = {i: (4 - i) % 16 for i in range(16)}
OFFSETS = ((0, 12), (4, 8))


def total(value):
    return jnp.sum(jnp.sum(value, axis=0, keepdims=True), axis=1, keepdims=True)


def kernel(
    near_row, near_col, far_row, far_col, far_rank,
    rhs, self_term, near_hbm, left_hbm, right_hbm,
    solution_out, basis_out,
    near, left, right, load_sem,
    own, along, along_send, along_recv,
    plane, plane_send, plane_recv,
    whole, gather_send, gather_recv, core_send, core_recv,
    terms, terms_send, terms_recv,
    tile, tile_send, tile_recv,
    sums, sums_send, sums_recv, pair, pair_send, pair_recv,
    hot, flat_rhs, flat_self, flat_along, pick,
):
    r = lax.axis_index("rows")
    b = lax.axis_index("bal")
    z, c = r // 2, r % 2
    x, y = b // 4, b % 4

    def along_z(i):
        return (((z + i + 16) % 16) * 2 + c, b)

    def in_plane(j):
        jx, jy = j // 4, j % 4
        px = x + jx - 2 * (x % 2) * (jx % 2) - 4 * ((x // 2) * (jx // 2))
        py = y + jy - 2 * (y % 2) * (jy % 2) - 4 * ((y // 2) * (jy // 2))
        return px * 4 + py

    sibling = (z * 2 + 1 - c, b)
    peer = {j: in_plane(j) for j in PLANE}

    barrier = pltpu.get_barrier_semaphore()
    for i in ALONG:
        pl.semaphore_signal(barrier, inc=1, device_id=along_z(i), device_id_type=MESH)
    for j in PLANE:
        pl.semaphore_signal(barrier, inc=1, device_id=(r, peer[j]), device_id_type=MESH)
    pl.semaphore_signal(barrier, inc=1, device_id=sibling, device_id_type=MESH)

    loads = [
        pltpu.make_async_copy(a, v, load_sem.at[n])
        for n, (a, v) in enumerate(((near_hbm, near), (left_hbm, left), (right_hbm, right)))
    ]
    for load in loads:
        load.start()

    def halves(value):
        return jnp.concatenate([value[:, :128], value[:, 128:]], axis=0)

    own_rhs = halves(rhs[...])
    own[...] = own_rhs
    along[4] = own_rhs

    base = r * 32
    lane = lax.broadcasted_iota(jnp.int32, (4, 128), 0) * 128 + lax.broadcasted_iota(jnp.int32, (4, 128), 1)
    mine = (lane // 16) % 16 == b
    half_of = (lane // 8) % 2
    task_of = lane % 8 + 8 * (lane // 256)
    row_of = jnp.full((4, 128), -1, jnp.int32)
    for k in range(NEAR + FARS):
        local = (near_row[k] if k < NEAR else far_row[k - NEAR]) - base
        row_of = jnp.where(mine & (task_of == k), 2 * local - local % 2, row_of)
    place = jnp.where(row_of >= 0, row_of + 2 * half_of + 1, 0).astype(F32)
    plane[b] = jnp.concatenate([own_rhs, halves(self_term[...]), place, jnp.zeros((4, 128), F32)], axis=0)

    pl.semaphore_wait(barrier, 31)

    pending = []

    def send(src, dst, send_sem, recv_sem, device):
        copy = pltpu.make_async_remote_copy(
            src_ref=src, dst_ref=dst, send_sem=send_sem, recv_sem=recv_sem, device_id=device, device_id_type=MESH
        )
        copy.start()
        pending.append(copy)

    def arrived(dst, recv_sem):
        pltpu.make_async_remote_copy(
            src_ref=dst, dst_ref=dst, send_sem=recv_sem, recv_sem=recv_sem, device_id=sibling, device_id_type=MESH
        ).wait_recv()

    for i in ALONG:
        send(own, along.at[SLOT[i]], along_send.at[i], along_recv.at[SLOT[i]], along_z(i))
    for j in PLANE:
        send(plane.at[b], plane.at[b], plane_send.at[j], plane_recv.at[j], (r, peer[j]))

    task = lax.broadcasted_iota(jnp.int32, (32, 1), 0)
    half = task // 16
    place_1 = jnp.full((32, 1), -1, jnp.int32)
    place_2 = jnp.full((32, 1), -1, jnp.int32)
    for k in range(NEAR + FARS):
        col = near_col[k] if k < NEAR else far_col[k - NEAR]
        other = jnp.where((col // 32) % 2 == c, 0, 1)
        d = (col // 64 - z + 16) % 16
        dev = (col % 32) // 2
        cl = col % 2
        e = (d + 4) % 16
        p1 = (((other * 2 + e // 8) * 16 + dev) * 2 + (e // 4) % 2) * 16 + (e % 4) * 4 + cl
        m = d // 4
        batch = jnp.where((m == 1) | (m == 2), 1, 0)
        holder = (d % 4) * 4 + dev // 4
        p2 = (((other * 2 + batch) * 16 + holder) * 2 + m // 2) * 16 + (dev % 4) * 4 + cl
        place_1 = jnp.where(task % 16 == k, p1 + 2 * half, place_1)
        place_2 = jnp.where(task % 16 == k, p2 + 2 * half, place_2)
    spot = lax.broadcasted_iota(jnp.int32, (32, 512), 1)
    for g in range(4):
        hot[0, g] = jnp.where(spot + 512 * g == place_1, 1.0, 0.0).astype(BF16)
        hot[1, g] = jnp.where(spot + 512 * g == place_2, 1.0, 0.0).astype(BF16)

    rank_of = jnp.zeros((16, 1), jnp.int32)
    task16 = lax.broadcasted_iota(jnp.int32, (16, 1), 0)
    for k in range(FARS):
        rank_of = jnp.where(task16 == NEAR + k, far_rank[k], rank_of)
    lane192 = lax.broadcasted_iota(jnp.int32, (16, FARS * RANK), 1)
    keep = (lane192 // RANK + NEAR == task16) & (lane192 % RANK < rank_of)

    def send_batch(it, batch):
        for j in PLANE:
            part = whole.at[it, 0, batch, b]
            send(part, part, gather_send.at[it, batch, j], gather_recv.at[it, batch, j], (r, peer[j]))

    def finish_batch(it, batch):
        for j in PLANE:
            arrived(whole.at[it, 0, batch, peer[j]], gather_recv.at[it, batch, j])
        send(whole.at[it, 0, batch], whole.at[it, 1, batch], core_send.at[it, batch], core_recv.at[it, batch], sibling)

    def picked(it, other, batch):
        source = whole[it, other, batch].reshape(512, 128)
        return jnp.dot(hot[it, other * 2 + batch], source, preferred_element_type=F32)

    def joined(value):
        return jnp.concatenate([value[:16], value[16:]], axis=1)

    def send_terms(it, kind, value):
        terms[it, kind, b] = halves(value).astype(BF16)
        for j in PLANE:
            part = terms.at[it, kind, b]
            send(part, part, terms_send.at[it, kind, j], terms_recv.at[it, kind, j], (r, peer[j]))

    def take_terms(it, kind, select):
        for j in PLANE:
            arrived(terms.at[it, kind, peer[j]], terms_recv.at[it, kind, j])
        return jnp.dot(select, terms[it, kind].reshape(256, 128), preferred_element_type=F32)

    def near_terms(picks):
        source = joined(picks)
        out = jnp.zeros((16, 256), F32)
        for k in range(NEAR):
            one = jnp.where(task16 == k, source, 0.0).astype(BF16)
            out += lax.dot_general(one, near[k], (((1,), (1,)), ((), ())), preferred_element_type=F32)
        return out[:8]

    def far_terms(picks):
        source = joined(picks).astype(BF16)
        coeff = lax.dot_general(
            source, right[...].reshape(FARS * RANK, 256), (((1,), (1,)), ((), ())), preferred_element_type=F32
        )
        coeff = jnp.where(keep, coeff, 0.0).astype(BF16)
        return jnp.dot(coeff, left[...].reshape(FARS * RANK, 256), preferred_element_type=F32)[8:]

    def send_sums(stage, values):
        lanes = lax.broadcasted_iota(jnp.int32, (1, 128), 1)
        row = jnp.zeros((1, 128), F32)
        for n, value in enumerate(values):
            row = jnp.where(lanes == n, value, row)
        sums[stage, z] = row
        for i in ALONG:
            part = sums.at[stage, z]
            send(part, part, sums_send.at[stage, i], sums_recv.at[stage, i], along_z(i))

    def pair_sums(stage):
        for i in ALONG:
            arrived(sums.at[stage, (z - i + 16) % 16], sums_recv.at[stage, i])
        pair[stage, 0] = jnp.sum(sums[stage], axis=0)
        send(pair.at[stage, 0], pair.at[stage, 1], pair_send.at[stage], pair_recv.at[stage], sibling)

    def take_sums(stage, count):
        arrived(pair.at[stage, 1], pair_recv.at[stage])
        row = pair[stage, 0] + pair[stage, 1]
        return [row[:, n : n + 1] for n in range(count)]

    def along_batch(batch):
        for e in range(8 * batch, 8 * batch + 8):
            if e != 4:
                arrived(along.at[e], along_recv.at[e])
            flat_along[4 * e : 4 * e + 4] = along[e]
        part = flat_along[32 * batch : 32 * batch + 32].astype(BF16)
        whole[0, 0, batch, b] = part.reshape(2, 16, 128)
        send_batch(0, batch)

    along_batch(0)
    for j in PLANE:
        arrived(plane.at[peer[j]], plane_recv.at[j])
    index = jnp.zeros((4, 128), F32)
    for dev in range(16):
        flat_rhs[4 * dev : 4 * dev + 4] = plane[dev, 0:4]
        flat_self[4 * dev : 4 * dev + 4] = plane[dev, 4:8]
        index += plane[dev, 8:12]
    index = index.astype(jnp.int32)
    spots = lax.broadcasted_iota(jnp.int32, (64, 256), 0) + 1
    selects = [
        jnp.where(
            spots == jnp.concatenate([index[2 * kind : 2 * kind + 1], index[2 * kind + 1 : 2 * kind + 2]], axis=1),
            1.0, 0.0,
        ).astype(BF16)
        for kind in range(2)
    ]
    squares = flat_rhs[...] * flat_rhs[...]
    send_sums(0, [total(squares), total(squares * flat_self[...])])
    along_batch(1)

    def operate(it, before_far):
        finish_batch(it, 0)
        picks = picked(it, 0, 0)
        arrived(whole.at[it, 1, 0], core_recv.at[it, 0])
        picks += picked(it, 1, 0)
        if it == 0:
            for load in loads:
                load.wait()
        send_terms(it, 0, near_terms(picks))
        pick[...] = picks
        if it == 1:
            before_far()
        finish_batch(it, 1)
        picks = pick[...] + picked(it, 0, 1)
        if it == 0:
            before_far()
        arrived(whole.at[it, 1, 1], core_recv.at[it, 1])
        picks += picked(it, 1, 1)
        send_terms(it, 1, far_terms(picks))
        out = take_terms(it, 0, selects[0])
        return out + take_terms(it, 1, selects[1])

    image = operate(0, lambda: pair_sums(0))
    beta_squared, diagonal = take_sums(0, 2)
    beta = jnp.sqrt(beta_squared)
    guess = diagonal / beta_squared
    first = flat_rhs[...] / beta
    image = (flat_self[...] * flat_rhs[...] + image) / beta
    shifted = image - guess * first

    tile[...] = shifted.astype(BF16).reshape(4, 16, 128)

    def tile_copy(batch, n):
        number = batch * 2 + n
        part = whole.at[1, 0, batch, b, n]
        source = (z - x - OFFSETS[batch][n] + 32) % 16
        return pltpu.make_async_remote_copy(
            src_ref=tile.at[y], dst_ref=part, send_sem=tile_send.at[number], recv_sem=tile_recv.at[number],
            device_id=(source * 2 + c, b), device_id_type=MESH,
        )

    for batch, n in ((1, 1), (1, 0), (0, 1)):
        tile_copy(batch, n).start()

    @pl.when(x > 0)
    def _():
        tile_copy(0, 0).start()

    @pl.when(x == 0)
    def _():
        whole[1, 0, 0, b, 0] = tile[y]

    send_sums(1, [total(first * first), total(first * shifted), total(shifted * shifted)])

    @pl.when(x > 0)
    def _():
        tile_copy(0, 0).wait_recv()

    tile_copy(0, 1).wait_recv()
    send_batch(1, 0)
    tile_copy(1, 0).wait_recv()
    tile_copy(1, 1).wait_recv()
    send_batch(1, 1)

    second = operate(1, lambda: pair_sums(1))
    g11, p1, p2 = take_sums(1, 3)
    h11 = guess * g11 + p1
    step = h11 - guess
    h21 = jnp.sqrt(jnp.maximum(p2 - 2.0 * step * p1 + step * step * g11, 0.0) + 1e-06)
    second = (flat_self[...] * shifted + second - step * image) / h21
    basis = (shifted - step * first) / h21
    rest = second - guess * basis
    send_sums(
        2,
        [total(first * rest), total(basis * rest), total(rest * rest), total(first * basis), total(basis * basis)],
    )

    def mine_of(value):
        flat_along[...] = value
        two = flat_along[pl.ds(pl.multiple_of((b // 2) * 8, 8), 8), :]
        return jnp.where(b % 2 == 0, two[:4], two[4:])

    own_first, own_basis, own_rest = mine_of(first), mine_of(basis), mine_of(rest)

    pair_sums(2)
    q1, q2, q3, g12, g22 = take_sums(2, 5)
    h12 = q1 + guess * g12
    h22 = q2 + guess * g22
    left_over = h22 - guess
    square = (
        q3 - 2.0 * h12 * q1 - 2.0 * left_over * q2
        + h12 * h12 * g11 + left_over * left_over * g22 + 2.0 * h12 * left_over * g12
    )
    h32 = jnp.sqrt(jnp.maximum(square, 0.0) + 1e-06)

    radius = jnp.sqrt(h11 * h11 + h21 * h21)
    cosine = h11 / radius
    sine = h21 / radius
    upper = cosine * h12 + sine * h22
    lower = cosine * h22 - sine * h12
    radius_two = jnp.sqrt(lower * lower + h32 * h32)
    coef_two = -(lower / radius_two) * sine * beta / radius_two
    coef_one = (cosine * beta - upper * coef_two) / radius

    def put(out, value):
        out[...] = jnp.concatenate([value[0:2], value[2:4]], axis=1)

    put(solution_out, coef_one * own_first + coef_two * own_basis)
    put(basis_out, (own_rest - h12 * own_first - left_over * own_basis) / h32)

    for copy in pending:
        copy.wait_send()
    for batch, n in ((1, 1), (1, 0), (0, 1)):
        tile_copy(batch, n).wait_send()

    @pl.when(x > 0)
    def _():
        tile_copy(0, 0).wait_send()


def shards(rhs, self_term, near_blocks, near_row, near_col, far_left, far_right, far_row, far_col, far_rank):
    vmem = pl.BlockSpec(memory_space=pltpu.VMEM)
    smem = pl.BlockSpec(memory_space=pltpu.SMEM)
    anywhere = pl.BlockSpec(memory_space=pl.ANY)
    dma = pltpu.SemaphoreType.DMA
    return pl.pallas_call(
        kernel,
        out_shape=[jax.ShapeDtypeStruct(rhs.shape, F32)] * 2,
        in_specs=[smem] * 5 + [vmem] * 2 + [anywhere] * 3,
        out_specs=[vmem] * 2,
        scratch_shapes=[
            pltpu.VMEM(near_blocks.shape, BF16), pltpu.VMEM(far_left.shape, BF16), pltpu.VMEM(far_right.shape, BF16),
            dma((3,)),
            pltpu.VMEM((4, 128), F32), pltpu.VMEM((16, 4, 128), F32), dma((16,)), dma((16,)),
            pltpu.VMEM((16, 16, 128), F32), dma((16,)), dma((16,)),
            pltpu.VMEM((2, 2, 2, 16, 2, 16, 128), BF16), dma((2, 2, 16)), dma((2, 2, 16)), dma((2, 2)), dma((2, 2)),
            pltpu.VMEM((2, 2, 16, 16, 128), BF16), dma((2, 2, 16)), dma((2, 2, 16)),
            pltpu.VMEM((4, 16, 128), BF16), dma((4,)), dma((4,)),
            pltpu.VMEM((3, 16, 1, 128), F32), dma((3, 16)), dma((3, 16)),
            pltpu.VMEM((3, 2, 1, 128), F32), dma((3,)), dma((3,)),
            pltpu.VMEM((2, 4, 32, 512), BF16), pltpu.VMEM((64, 128), F32), pltpu.VMEM((64, 128), F32),
            pltpu.VMEM((64, 128), F32), pltpu.VMEM((32, 128), F32),
        ],
        compiler_params=pltpu.CompilerParams(
            collective_id=0, has_side_effects=True, vmem_limit_bytes=24 * 1024 * 1024
        ),
        name="gmres",
    )(near_row, near_col, far_row, far_col, far_rank, rhs, self_term, near_blocks, far_left, far_right)


def solution(mesh):
    vec = P(("rows", "bal"), None)
    blocks = P(("rows", "bal"), None, None)
    ints = P(("rows", "bal"))
    in_specs = (vec, vec, blocks, ints, ints, blocks, blocks, ints, ints, ints)
    return jax.shard_map(shards, mesh=mesh, in_specs=in_specs, out_specs=(vec, vec), check_vma=False)
```

```python
import jax
import jax.numpy as jnp
from jax import lax
from jax.experimental import pallas as pl
from jax.experimental.pallas import tpu as pltpu
from jax.sharding import PartitionSpec as P

MESH = pl.DeviceIdType.MESH
F32 = jnp.float32
BF16 = jnp.bfloat16
NEAR, FARS, RANK = 8, 6, 32

RING_HOPS = (0, 1, 2, 1)
PLANE = sorted(range(1, 16), key=lambda j: -(RING_HOPS[j // 4] + RING_HOPS[j % 4]))
ALONG = sorted(range(1, 16), key=lambda i: -min(i, 16 - i))


def signed(i):
    return i if i <= 8 else i - 16


def ranked(d):
    return 2 * abs(d) - (d > 0)


RANKS = {i: ranked(signed(-i % 16)) for i in ALONG}
BOUNDS = ((0, 4, 3), (4, 12, 8), (12, 20, 8))


def total(value):
    return jnp.sum(jnp.sum(value, axis=0, keepdims=True), axis=1, keepdims=True)


def kernel(
    near_row_hbm, near_col_hbm, far_row_hbm, far_col_hbm, far_rank_hbm,
    rhs_hbm, self_hbm, near_hbm, left_hbm, right_hbm,
    out,
    near_row, near_col, far_row, far_col, far_rank, rhs, self_term,
    near, left, right, load_sem,
    own, along, along_send, along_recv,
    plane, plane_send, plane_recv,
    first_tiles, middle_tiles, last_tiles, gather_send, gather_recv, core_send, core_recv,
    terms, terms_send, terms_recv,
    tile, tile_send, tile_recv,
    sums, sums_send, sums_recv, pair, pair_send, pair_recv,
    hot_first, hot_middle, hot_last, flat_rhs, flat_self, flat_along, pick,
):
    r = lax.axis_index("rows")
    b = lax.axis_index("bal")
    z, c = r // 2, r % 2
    x, y = b // 4, b % 4

    def along_z(i, core=c):
        return (((z + i + 16) % 16) * 2 + core, b)

    def in_plane(j):
        jx, jy = j // 4, j % 4
        px = x + jx - 2 * (x % 2) * (jx % 2) - 4 * ((x // 2) * (jx // 2))
        py = y + jy - 2 * (y % 2) * (jy % 2) - 4 * ((y // 2) * (jy // 2))
        return px * 4 + py

    sibling = (z * 2 + 1 - c, b)
    peer = {j: in_plane(j) for j in PLANE}
    both = [i for i in ALONG if RANKS[i] > 8]

    barrier = pltpu.get_barrier_semaphore()
    for i in ALONG:
        pl.semaphore_signal(barrier, inc=1, device_id=along_z(i), device_id_type=MESH)
    for i in both:
        pl.semaphore_signal(barrier, inc=1, device_id=along_z(i, 1 - c), device_id_type=MESH)
    for j in PLANE:
        pl.semaphore_signal(barrier, inc=1, device_id=(r, peer[j]), device_id_type=MESH)
    pl.semaphore_signal(barrier, inc=1, device_id=sibling, device_id_type=MESH)

    loads = [
        pltpu.make_async_copy(a, v, load_sem.at[n])
        for n, (a, v) in enumerate(
            (
                (rhs_hbm, rhs), (self_hbm, self_term), (near_row_hbm, near_row), (far_row_hbm, far_row),
                (near_col_hbm, near_col), (far_col_hbm, far_col), (far_rank_hbm, far_rank),
                (near_hbm, near), (left_hbm, left), (right_hbm, right),
            )
        )
    ]
    for load in loads:
        load.start()
    for load in loads[:7]:
        load.wait()

    def halves(value):
        return jnp.concatenate([value[:, :128], value[:, 128:]], axis=0)

    own_rhs = halves(rhs[...])
    own[...] = own_rhs
    along[0] = own_rhs

    base = r * 32
    lane = lax.broadcasted_iota(jnp.int32, (4, 128), 0) * 128 + lax.broadcasted_iota(jnp.int32, (4, 128), 1)
    mine = ((lane >> 4) & 15) == b
    half_of = (lane >> 3) & 1
    task_of = (lane & 7) + 8 * (lane >> 8)
    row_of = jnp.full((4, 128), -1, jnp.int32)
    for k in range(NEAR + FARS):
        local = (near_row[k] if k < NEAR else far_row[k - NEAR]) - base
        row_of = jnp.where(mine & (task_of == k), 2 * local - (local & 1), row_of)
    place = jnp.where(row_of >= 0, row_of + 2 * half_of + 1, 0).astype(F32)
    plane[b] = jnp.concatenate([own_rhs, halves(self_term[...]), place, jnp.zeros((4, 128), F32)], axis=0)

    pl.semaphore_wait(barrier, 31 + len(both))

    pending = []

    def send(src, dst, send_sem, recv_sem, device):
        pltpu.make_async_remote_copy(
            src_ref=src, dst_ref=dst, send_sem=send_sem, recv_sem=recv_sem, device_id=device, device_id_type=MESH
        ).start()

    def whole_stage(ref, send_sem, recv_sem):
        return pltpu.make_async_remote_copy(
            src_ref=ref, dst_ref=ref, send_sem=send_sem, recv_sem=recv_sem, device_id=sibling, device_id_type=MESH
        )

    def arrived(ref, recv_sem):
        whole_stage(ref, recv_sem, recv_sem).wait_recv()

    def sending(ref, send_sem):
        pending.append(whole_stage(ref, send_sem, send_sem))

    def settle():
        while pending:
            pending.pop().wait_send()

    for i in ALONG:
        rank = RANKS[i]
        batch = (rank // 4 + 1) // 2
        send(own, along.at[rank], along_send.at[0], along_recv.at[batch], along_z(i))
        if batch == 2:
            send(own, along.at[rank + 4], along_send.at[0], along_recv.at[batch], along_z(i, 1 - c))
    sending(along.at[0:19], along_send.at[0])
    for j in PLANE:
        send(plane.at[b], plane.at[b], plane_send.at[0], plane_recv.at[0], (r, peer[j]))
    sending(plane.at[0:15], plane_send.at[0])

    task = lax.broadcasted_iota(jnp.int32, (32, 1), 0)
    half = task >> 4
    place_1 = jnp.full((32, 1), -1, jnp.int32)
    place_2 = jnp.full((32, 1), -1, jnp.int32)
    for k in range(NEAR + FARS):
        col = near_col[k] if k < NEAR else far_col[k - NEAR]
        other = ((col >> 5) & 1) ^ c
        d = ((col >> 6) - z + 16) & 15
        dev = (col >> 1) & 15
        cl = col & 1
        rank = jnp.where(d == 0, 0, jnp.where(d <= 8, 2 * d - 1, 32 - 2 * d))
        tile_of, low = rank >> 2, rank & 3

        def spot_of(holder, row):
            in_first = other * 256 + holder * 16 + row
            in_middle = 512 + other * 512 + holder * 32 + (tile_of - 1) * 16 + row
            in_last = 1536 + holder * 32 + other * 16 + row
            return jnp.where(tile_of == 0, in_first, jnp.where(tile_of == 3, in_last, in_middle))

        p1 = spot_of(dev, low * 4 + cl)
        p2 = spot_of(low * 4 + (dev >> 2), (dev & 3) * 4 + cl)
        place_1 = jnp.where((task & 15) == k, p1 + 2 * half, place_1)
        place_2 = jnp.where((task & 15) == k, p2 + 2 * half, place_2)
    spot = lax.broadcasted_iota(jnp.int32, (32, 512), 1)

    def hots(place, start, size):
        return jnp.where(spot[:, :size] + start == place, 1.0, 0.0).astype(BF16)

    for it, place in ((0, place_1), (1, place_2)):
        for other in range(2):
            hot_first[it, other] = hots(place, 256 * other, 256)
            hot_middle[it, other] = hots(place, 512 + 512 * other, 512)
        hot_last[it] = hots(place, 1536, 512)

    rank_of = jnp.zeros((16, 1), jnp.int32)
    task16 = lax.broadcasted_iota(jnp.int32, (16, 1), 0)
    for k in range(FARS):
        rank_of = jnp.where(task16 == NEAR + k, far_rank[k], rank_of)
    lane192 = lax.broadcasted_iota(jnp.int32, (16, FARS * RANK), 1)
    keep = ((lane192 >> 5) + NEAR == task16) & ((lane192 & 31) < rank_of)

    own_tiles = [[first_tiles.at[it, 0], middle_tiles.at[it, 0], last_tiles.at[it]] for it in range(2)]

    def send_batch(it, batch):
        held = own_tiles[it][batch]
        for j in PLANE:
            part = held.at[b]
            send(part, part, gather_send.at[it, batch], gather_recv.at[it, batch], (r, peer[j]))
        sending(held.at[0:15], gather_send.at[it, batch])

    def finish_batch(it, batch):
        held = own_tiles[it][batch]
        arrived(held.at[0:15], gather_recv.at[it, batch])
        if batch < 2:
            there = (first_tiles, middle_tiles)[batch].at[it, 1]
            send(held, there, core_send.at[it, batch], core_recv.at[it, batch], sibling)
            sending(held, core_send.at[it, batch])

    def picked(hot, source):
        return jnp.dot(hot, source.reshape(-1, 128), preferred_element_type=F32)

    def joined(value):
        return jnp.concatenate([value[:16], value[16:]], axis=1)

    def send_terms(it, kind, value):
        terms[it, kind, b] = halves(value).astype(BF16)
        for j in PLANE:
            part = terms.at[it, kind, b]
            send(part, part, terms_send.at[it, kind], terms_recv.at[it, kind], (r, peer[j]))
        sending(terms.at[it, kind, 0:15], terms_send.at[it, kind])

    def take_terms(it, kind, select):
        arrived(terms.at[it, kind, 0:15], terms_recv.at[it, kind])
        return jnp.dot(select, terms[it, kind].reshape(256, 128), preferred_element_type=F32)

    def near_terms(picks):
        source = joined(picks)
        result = jnp.zeros((16, 256), F32)
        for k in range(NEAR):
            one = jnp.where(task16 == k, source, 0.0).astype(BF16)
            result += lax.dot_general(one, near[k], (((1,), (1,)), ((), ())), preferred_element_type=F32)
        return result[:8]

    def far_terms(picks):
        source = joined(picks).astype(BF16)
        coeff = lax.dot_general(
            source, right[...].reshape(FARS * RANK, 256), (((1,), (1,)), ((), ())), preferred_element_type=F32
        )
        coeff = jnp.where(keep, coeff, 0.0).astype(BF16)
        return jnp.dot(coeff, left[...].reshape(FARS * RANK, 256), preferred_element_type=F32)[8:]

    def send_sums(stage, values):
        lanes = lax.broadcasted_iota(jnp.int32, (1, 128), 1)
        row = jnp.zeros((1, 128), F32)
        for n, value in enumerate(values):
            row = jnp.where(lanes == n, value, row)
        sums[stage, 0] = row
        for i in ALONG:
            slot = RANKS[i]
            far = int(slot > 8)
            send(sums.at[stage, 0], sums.at[stage, slot], sums_send.at[stage], sums_recv.at[stage, far], along_z(i))
            if far and stage == 2:
                there = sums.at[stage, slot + 7]
                send(sums.at[stage, 0], there, sums_send.at[stage], sums_recv.at[stage, 1], along_z(i, 1 - c))
        sending(sums.at[stage, 0 : 22 if stage == 2 else 15], sums_send.at[stage])

    def pair_sums(stage):
        arrived(sums.at[stage, 0:8], sums_recv.at[stage, 0])
        if stage < 2:
            arrived(sums.at[stage, 0:7], sums_recv.at[stage, 1])
        pair[stage, 0] = jnp.sum(sums[stage, 0 : 9 if stage == 2 else 16], axis=0)
        send(pair.at[stage, 0], pair.at[stage, 1], pair_send.at[stage], pair_recv.at[stage], sibling)
        sending(pair.at[stage, 0], pair_send.at[stage])

    def take_sums(stage, count):
        arrived(pair.at[stage, 1], pair_recv.at[stage])
        row = pair[stage, 0] + pair[stage, 1]
        if stage == 2:
            arrived(sums.at[stage, 0:14], sums_recv.at[stage, 1])
            row += jnp.sum(sums[stage, 9:23], axis=0)
        return [row[:, n : n + 1] for n in range(count)]

    for batch, (start, stop, count) in enumerate(BOUNDS):
        arrived(along.at[0:count], along_recv.at[batch])
        for e in range(start, stop):
            flat_along[4 * e : 4 * e + 4] = along[e]
        part = flat_along[4 * start : 4 * stop].astype(BF16)
        own_tiles[0][batch][b] = part if batch == 0 else part.reshape(2, 16, 128)
        send_batch(0, batch)

    arrived(plane.at[0:15], plane_recv.at[0])
    index = jnp.zeros((4, 128), F32)
    for dev in range(16):
        flat_rhs[4 * dev : 4 * dev + 4] = plane[dev, 0:4]
        flat_self[4 * dev : 4 * dev + 4] = plane[dev, 4:8]
        index += plane[dev, 8:12]
    squares = flat_rhs[...] * flat_rhs[...]
    send_sums(0, [total(squares), total(squares * flat_self[...])])
    index = index.astype(jnp.int32)
    spots = lax.broadcasted_iota(jnp.int32, (64, 256), 0) + 1
    selects = [
        jnp.where(
            spots == jnp.concatenate([index[2 * kind : 2 * kind + 1], index[2 * kind + 1 : 2 * kind + 2]], axis=1),
            1.0, 0.0,
        ).astype(BF16)
        for kind in range(2)
    ]

    def operate(it):
        finish_batch(it, 0)
        picks = picked(hot_first[it, 0], first_tiles[it, 0])
        arrived(first_tiles.at[it, 1], core_recv.at[it, 0])
        picks += picked(hot_first[it, 1], first_tiles[it, 1])
        if it == 0:
            for load in loads[7:]:
                load.wait()
        send_terms(it, 0, near_terms(picks))
        pick[...] = picks
        finish_batch(it, 1)
        picks = pick[...] + picked(hot_middle[it, 0], middle_tiles[it, 0])
        arrived(middle_tiles.at[it, 1], core_recv.at[it, 1])
        picks += picked(hot_middle[it, 1], middle_tiles[it, 1])
        finish_batch(it, 2)
        picks += picked(hot_last[it], last_tiles[it])
        send_terms(it, 1, far_terms(picks))
        pair_sums(it)
        image = take_terms(it, 0, selects[0])
        return image + take_terms(it, 1, selects[1])

    image = operate(0)
    beta_squared, diagonal = take_sums(0, 2)
    beta = jnp.sqrt(beta_squared)
    guess = diagonal / beta_squared
    inverse = 1.0 / beta
    first = flat_rhs[...] * inverse
    image = (flat_self[...] * flat_rhs[...] + image) * inverse
    shifted = image - guess * first

    tile[...] = shifted.astype(BF16).reshape(4, 16, 128)

    def tile_copy(n, core=0):
        rank = 4 * n + x
        away = (rank + 1) // 2
        d = away * (2 * (rank % 2) - 1)
        held = own_tiles[1][(n + 1) // 2].at[b]
        part = held if n == 0 else held.at[n - 1] if n < 3 else held.at[core]
        return pltpu.make_async_remote_copy(
            src_ref=tile.at[y], dst_ref=part, send_sem=tile_send.at[n + core], recv_sem=tile_recv.at[n + core],
            device_id=along_z(-d, 1 - c if core else c), device_id_type=MESH,
        )

    far_tiles = [tile_copy(3), tile_copy(3, 1), tile_copy(2), tile_copy(1)]
    for copy in far_tiles:
        copy.start()

    @pl.when(x > 0)
    def _():
        tile_copy(0).start()

    @pl.when(x == 0)
    def _():
        first_tiles[1, 0, b] = tile[y]

    send_sums(1, [total(first * first), total(first * shifted), total(shifted * shifted)])

    @pl.when(x > 0)
    def _():
        tile_copy(0).wait_recv()

    send_batch(1, 0)
    far_tiles[3].wait_recv()
    far_tiles[2].wait_recv()
    send_batch(1, 1)
    far_tiles[0].wait_recv()
    far_tiles[1].wait_recv()
    send_batch(1, 2)

    second = operate(1)
    g11, p1, p2 = take_sums(1, 3)
    h11 = guess * g11 + p1
    step = h11 - guess
    h21 = jnp.sqrt(jnp.maximum(p2 - 2.0 * step * p1 + step * step * g11, 0.0) + 1e-06)
    inverse = 1.0 / h21
    second = (flat_self[...] * shifted + second - step * image) * inverse
    basis = (shifted - step * first) * inverse
    rest = second - guess * basis
    send_sums(
        2,
        [total(first * rest), total(basis * rest), total(rest * rest), total(first * basis), total(basis * basis)],
    )

    def mine_of(value):
        flat_along[0:64] = value
        two = flat_along[pl.ds(pl.multiple_of((b // 2) * 8, 8), 8), :]
        return jnp.where(b % 2 == 0, two[:4], two[4:])

    own_first, own_basis, own_rest = mine_of(first), mine_of(basis), mine_of(rest)
    for copy in far_tiles:
        copy.wait_send()

    @pl.when(x > 0)
    def _():
        tile_copy(0).wait_send()

    settle()

    pair_sums(2)
    q1, q2, q3, g12, g22 = take_sums(2, 5)
    h12 = q1 + guess * g12
    h22 = q2 + guess * g22
    left_over = h22 - guess
    square = (
        q3 - 2.0 * h12 * q1 - 2.0 * left_over * q2
        + h12 * h12 * g11 + left_over * left_over * g22 + 2.0 * h12 * left_over * g12
    )
    h32 = jnp.sqrt(jnp.maximum(square, 0.0) + 1e-06)

    radius = jnp.sqrt(h11 * h11 + h21 * h21)
    cosine = h11 / radius
    sine = h21 / radius
    upper = cosine * h12 + sine * h22
    lower = cosine * h22 - sine * h12
    radius_two = jnp.sqrt(lower * lower + h32 * h32)
    coef_two = -(lower / radius_two) * sine * beta / radius_two
    coef_one = (cosine * beta - upper * coef_two) / radius

    def wide(value):
        return jnp.concatenate([value[0:2], value[2:4]], axis=1)

    out[0] = wide(coef_one * own_first + coef_two * own_basis)
    out[1] = wide((own_rest - h12 * own_first - left_over * own_basis) / h32)

    settle()


def shards(rhs, self_term, near_blocks, near_row, near_col, far_left, far_right, far_row, far_col, far_rank):
    hbm = pl.BlockSpec(memory_space=pltpu.HBM)
    dma = pltpu.SemaphoreType.DMA
    out = pl.pallas_call(
        kernel,
        out_shape=jax.ShapeDtypeStruct((2, *rhs.shape), F32),
        in_specs=[hbm] * 10,
        out_specs=pl.BlockSpec(memory_space=pltpu.VMEM),
        scratch_shapes=[
            *[pltpu.SMEM(a.shape, jnp.int32) for a in (near_row, near_col, far_row, far_col, far_rank)],
            pltpu.VMEM(rhs.shape, F32), pltpu.VMEM(rhs.shape, F32),
            pltpu.VMEM(near_blocks.shape, BF16), pltpu.VMEM(far_left.shape, BF16), pltpu.VMEM(far_right.shape, BF16),
            dma((10,)),
            pltpu.VMEM((4, 128), F32), pltpu.VMEM((20, 4, 128), F32), dma((1,)), dma((3,)),
            pltpu.VMEM((16, 16, 128), F32), dma((1,)), dma((1,)),
            pltpu.VMEM((2, 2, 16, 16, 128), BF16), pltpu.VMEM((2, 2, 16, 2, 16, 128), BF16),
            pltpu.VMEM((2, 16, 2, 16, 128), BF16), dma((2, 3)), dma((2, 3)), dma((2, 2)), dma((2, 2)),
            pltpu.VMEM((2, 2, 16, 16, 128), BF16), dma((2, 2)), dma((2, 2)),
            pltpu.VMEM((4, 16, 128), BF16), dma((5,)), dma((5,)),
            pltpu.VMEM((3, 23, 1, 128), F32), dma((3,)), dma((3, 2)),
            pltpu.VMEM((3, 2, 1, 128), F32), dma((3,)), dma((3,)),
            pltpu.VMEM((2, 2, 32, 256), BF16), pltpu.VMEM((2, 2, 32, 512), BF16), pltpu.VMEM((2, 32, 512), BF16),
            pltpu.VMEM((64, 128), F32), pltpu.VMEM((64, 128), F32), pltpu.VMEM((80, 128), F32),
            pltpu.VMEM((32, 128), F32),
        ],
        compiler_params=pltpu.CompilerParams(
            collective_id=0, has_side_effects=True, vmem_limit_bytes=56 * 1024 * 1024
        ),
        name="gmres",
    )(near_row, near_col, far_row, far_col, far_rank, rhs, self_term, near_blocks, far_left, far_right)
    return out[0], out[1]


def solution(mesh):
    vec = P(("rows", "bal"), None)
    blocks = P(("rows", "bal"), None, None)
    ints = P(("rows", "bal"))
    in_specs = (vec, vec, blocks, ints, ints, blocks, blocks, ints, ints, ints)
    return jax.shard_map(shards, mesh=mesh, in_specs=in_specs, out_specs=(vec, vec), check_vma=False)
```

```python
import jax
import jax.numpy as jnp
from jax import lax
from jax.experimental import pallas as pl
from jax.experimental.pallas import tpu as pltpu
from jax.sharding import PartitionSpec as P

MESH = pl.DeviceIdType.MESH
F32 = jnp.float32
BF16 = jnp.bfloat16
NEAR, FARS, RANK = 8, 6, 32

RING_HOPS = (0, 1, 2, 1)
PLANE = sorted(range(1, 16), key=lambda j: -(RING_HOPS[j // 4] + RING_HOPS[j % 4]))
ALONG = sorted(range(1, 16), key=lambda i: -min(i, 16 - i))


def signed(i):
    return i if i <= 8 else i - 16


def ranked(d):
    return 2 * abs(d) - (d > 0)


RANKS = {i: ranked(signed(-i % 16)) for i in ALONG}
OFFSETS = ((0, 0), (0, 1), (2, 0), (0, 3), (1, 0), (1, 1), (3, 0), (3, 1))
BOUNDS = ((0, 4, 3), (4, 12, 8), (12, 20, 8))


def total(value):
    return jnp.sum(jnp.sum(value, axis=0, keepdims=True), axis=1, keepdims=True)


def kernel(
    near_row_hbm, near_col_hbm, far_row_hbm, far_col_hbm, far_rank_hbm,
    rhs_hbm, self_hbm, near_hbm, left_hbm, right_hbm,
    out,
    near_row, near_col, far_row, far_col, far_rank, rhs, self_term,
    near, left, right, load_sem,
    own, along, along_send, along_recv,
    plane, plane_send, plane_recv,
    first_1, middle_1, last_1, first_2, middle_2, last_2, gather_send, gather_recv, core_send, core_recv,
    terms, terms_send, terms_recv,
    tile, tile_send, tile_recv,
    sums, sums_send, sums_recv, pair, pair_send, pair_recv,
    hot_first, hot_middle, hot_last, flat_rhs, flat_self, flat_along, pick,
):
    r = lax.axis_index("rows")
    b = lax.axis_index("bal")
    z, c = r // 2, r % 2
    x, y = b // 4, b % 4

    def along_z(i, core=c):
        return (((z + i + 16) % 16) * 2 + core, b)

    def in_plane(j):
        jx, jy = j // 4, j % 4
        px = x + jx - 2 * (x % 2) * (jx % 2) - 4 * ((x // 2) * (jx // 2))
        py = y + jy - 2 * (y % 2) * (jy % 2) - 4 * ((y // 2) * (jy // 2))
        return px * 4 + py

    sibling = (z * 2 + 1 - c, b)
    peer = {j: in_plane(j) for j in PLANE}
    both = [i for i in ALONG if RANKS[i] > 8]

    barrier = pltpu.get_barrier_semaphore()
    for i in ALONG:
        pl.semaphore_signal(barrier, inc=1, device_id=along_z(i), device_id_type=MESH)
    for i in both:
        pl.semaphore_signal(barrier, inc=1, device_id=along_z(i, 1 - c), device_id_type=MESH)
    for j in PLANE:
        pl.semaphore_signal(barrier, inc=1, device_id=(r, peer[j]), device_id_type=MESH)
    pl.semaphore_signal(barrier, inc=1, device_id=sibling, device_id_type=MESH)

    loads = [
        pltpu.make_async_copy(a, v, load_sem.at[n])
        for n, (a, v) in enumerate(
            (
                (rhs_hbm, rhs), (self_hbm, self_term), (near_row_hbm, near_row), (far_row_hbm, far_row),
                (near_col_hbm, near_col), (far_col_hbm, far_col), (far_rank_hbm, far_rank),
                (near_hbm, near), (left_hbm, left), (right_hbm, right),
            )
        )
    ]
    for load in loads:
        load.start()
    for load in loads[:7]:
        load.wait()

    def halves(value):
        return jnp.concatenate([value[:, :128], value[:, 128:]], axis=0)

    own_rhs = halves(rhs[...])
    own[...] = own_rhs
    along[0] = own_rhs

    base = r * 32
    lane = lax.broadcasted_iota(jnp.int32, (4, 128), 0) * 128 + lax.broadcasted_iota(jnp.int32, (4, 128), 1)
    mine = ((lane >> 4) & 15) == b
    half_of = (lane >> 3) & 1
    task_of = (lane & 7) + 8 * (lane >> 8)
    row_of = jnp.full((4, 128), -1, jnp.int32)
    for k in range(NEAR + FARS):
        local = (near_row[k] if k < NEAR else far_row[k - NEAR]) - base
        row_of = jnp.where(mine & (task_of == k), 2 * local - (local & 1), row_of)
    place = jnp.where(row_of >= 0, row_of + 2 * half_of + 1, 0).astype(F32)
    plane[b] = jnp.concatenate([own_rhs, halves(self_term[...]), place, jnp.zeros((4, 128), F32)], axis=0)

    pl.semaphore_wait(barrier, 31 + len(both))

    pending = []

    def send(src, dst, send_sem, recv_sem, device):
        pltpu.make_async_remote_copy(
            src_ref=src, dst_ref=dst, send_sem=send_sem, recv_sem=recv_sem, device_id=device, device_id_type=MESH
        ).start()

    def whole_stage(ref, send_sem, recv_sem):
        return pltpu.make_async_remote_copy(
            src_ref=ref, dst_ref=ref, send_sem=send_sem, recv_sem=recv_sem, device_id=sibling, device_id_type=MESH
        )

    def arrived(ref, recv_sem):
        whole_stage(ref, recv_sem, recv_sem).wait_recv()

    def sending(ref, send_sem):
        pending.append(whole_stage(ref, send_sem, send_sem))

    def settle():
        while pending:
            pending.pop().wait_send()

    for i in ALONG:
        rank = RANKS[i]
        batch = (rank // 4 + 1) // 2
        send(own, along.at[rank], along_send.at[0], along_recv.at[batch], along_z(i))
        if batch == 2:
            send(own, along.at[rank + 4], along_send.at[0], along_recv.at[batch], along_z(i, 1 - c))
    sending(along.at[0:19], along_send.at[0])
    for j in PLANE:
        send(plane.at[b], plane.at[b], plane_send.at[0], plane_recv.at[0], (r, peer[j]))
    sending(plane.at[0:15], plane_send.at[0])

    task = lax.broadcasted_iota(jnp.int32, (32, 1), 0)
    half = task >> 4
    place_1 = jnp.full((32, 1), -1, jnp.int32)
    place_2 = jnp.full((32, 1), -1, jnp.int32)
    for k in range(NEAR + FARS):
        col = near_col[k] if k < NEAR else far_col[k - NEAR]
        other = ((col >> 5) & 1) ^ c
        d = ((col >> 6) - z + 16) & 15
        dev = (col >> 1) & 15
        cl = col & 1
        rank = jnp.where(d == 0, 0, jnp.where(d <= 8, 2 * d - 1, 32 - 2 * d))
        tile_of, low = rank >> 2, rank & 3

        row = low * 4 + cl
        in_first = other * 256 + dev * 16 + row
        in_middle = 512 + other * 512 + dev * 32 + (tile_of - 1) * 16 + row
        in_last = 1536 + dev * 32 + other * 16 + row
        p1 = jnp.where(tile_of == 0, in_first, jnp.where(tile_of == 3, in_last, in_middle))
        t = rank >> 1
        away = ((rank ^ t) & 1) ^ (x % 2)
        slot = away * 4 + (((dev >> 2) - y - 2 * (((x + away) & 3) >> 1) + 8) & 3)
        row = (dev & 3) * 4 + cl
        in_first = ((other * 8 + slot) * 2 + t) * 16 + row
        in_middle = 512 + ((other * 8 + slot) * 4 + t - 2) * 16 + row
        in_last = 1536 + ((slot * 2 + other) * 2 + t - 6) * 16 + row
        p2 = jnp.where(t < 2, in_first, jnp.where(t >= 6, in_last, in_middle))
        place_1 = jnp.where((task & 15) == k, p1 + 2 * half, place_1)
        place_2 = jnp.where((task & 15) == k, p2 + 2 * half, place_2)
    spot = lax.broadcasted_iota(jnp.int32, (32, 512), 1)

    def hots(place, start, size):
        return jnp.where(spot[:, :size] + start == place, 1.0, 0.0).astype(BF16)

    for it, place in ((0, place_1), (1, place_2)):
        for other in range(2):
            hot_first[it, other] = hots(place, 256 * other, 256)
            hot_middle[it, other] = hots(place, 512 + 512 * other, 512)
        hot_last[it] = hots(place, 1536, 512)

    rank_of = jnp.zeros((16, 1), jnp.int32)
    task16 = lax.broadcasted_iota(jnp.int32, (16, 1), 0)
    for k in range(FARS):
        rank_of = jnp.where(task16 == NEAR + k, far_rank[k], rank_of)
    lane192 = lax.broadcasted_iota(jnp.int32, (16, FARS * RANK), 1)
    keep = ((lane192 >> 5) + NEAR == task16) & ((lane192 & 31) < rank_of)

    own_tiles = [[first_1.at[0], middle_1.at[0], last_1], [first_2.at[0], middle_2.at[0], last_2]]
    other_tiles = [[first_1.at[1], middle_1.at[1]], [first_2.at[1], middle_2.at[1]]]

    def send_batch(it, batch):
        held = own_tiles[it][batch]
        if it == 0:
            for j in PLANE:
                send(held.at[b], held.at[b], gather_send.at[it, batch], gather_recv.at[it, batch], (r, peer[j]))
            sending(held.at[0:15], gather_send.at[it, batch])
        else:
            for slot in (2, 5, 7, 1, 3, 4, 6):
                ox, oy = OFFSETS[slot]
                to = (r, ((x - ox + 4) % 4) * 4 + (y - oy + 4) % 4)
                send(held.at[0], held.at[slot], gather_send.at[it, batch], gather_recv.at[it, batch], to)
            sending(held.at[0:7], gather_send.at[it, batch])

    def finish_batch(it, batch):
        held = own_tiles[it][batch]
        arrived(held.at[0 : 7 if it else 15], gather_recv.at[it, batch])
        if batch < 2:
            send(held, other_tiles[it][batch], core_send.at[it, batch], core_recv.at[it, batch], sibling)
            sending(held, core_send.at[it, batch])

    def picked(hot, source):
        return jnp.dot(hot, source.reshape(-1, 128), preferred_element_type=F32)

    def joined(value):
        return jnp.concatenate([value[:16], value[16:]], axis=1)

    def send_terms(it, kind, value):
        terms[it, kind, b] = halves(value).astype(BF16)
        for j in PLANE:
            part = terms.at[it, kind, b]
            send(part, part, terms_send.at[it, kind], terms_recv.at[it, kind], (r, peer[j]))
        sending(terms.at[it, kind, 0:15], terms_send.at[it, kind])

    def take_terms(it, kind, select):
        arrived(terms.at[it, kind, 0:15], terms_recv.at[it, kind])
        return jnp.dot(select, terms[it, kind].reshape(256, 128), preferred_element_type=F32)

    def near_terms(picks):
        source = joined(picks)
        result = jnp.zeros((16, 256), F32)
        for k in range(NEAR):
            one = jnp.where(task16 == k, source, 0.0).astype(BF16)
            result += lax.dot_general(one, near[k], (((1,), (1,)), ((), ())), preferred_element_type=F32)
        return result[:8]

    def far_terms(picks):
        source = joined(picks).astype(BF16)
        coeff = lax.dot_general(
            source, right[...].reshape(FARS * RANK, 256), (((1,), (1,)), ((), ())), preferred_element_type=F32
        )
        coeff = jnp.where(keep, coeff, 0.0).astype(BF16)
        return jnp.dot(coeff, left[...].reshape(FARS * RANK, 256), preferred_element_type=F32)[8:]

    def send_sums(stage, values):
        lanes = lax.broadcasted_iota(jnp.int32, (1, 128), 1)
        row = jnp.zeros((1, 128), F32)
        for n, value in enumerate(values):
            row = jnp.where(lanes == n, value, row)
        sums[stage, 0] = row
        for i in ALONG:
            slot = RANKS[i]
            far = int(slot > 8)
            send(sums.at[stage, 0], sums.at[stage, slot], sums_send.at[stage], sums_recv.at[stage, far], along_z(i))
            if far and stage == 2:
                there = sums.at[stage, slot + 7]
                send(sums.at[stage, 0], there, sums_send.at[stage], sums_recv.at[stage, 1], along_z(i, 1 - c))
        sending(sums.at[stage, 0 : 22 if stage == 2 else 15], sums_send.at[stage])

    def pair_sums(stage):
        arrived(sums.at[stage, 0:8], sums_recv.at[stage, 0])
        if stage < 2:
            arrived(sums.at[stage, 0:7], sums_recv.at[stage, 1])
        pair[stage, 0] = jnp.sum(sums[stage, 0 : 9 if stage == 2 else 16], axis=0)
        send(pair.at[stage, 0], pair.at[stage, 1], pair_send.at[stage], pair_recv.at[stage], sibling)
        sending(pair.at[stage, 0], pair_send.at[stage])

    def take_sums(stage, count):
        arrived(pair.at[stage, 1], pair_recv.at[stage])
        row = pair[stage, 0] + pair[stage, 1]
        if stage == 2:
            arrived(sums.at[stage, 0:14], sums_recv.at[stage, 1])
            row += jnp.sum(sums[stage, 9:23], axis=0)
        return [row[:, n : n + 1] for n in range(count)]

    for batch, (start, stop, count) in enumerate(BOUNDS):
        arrived(along.at[0:count], along_recv.at[batch])
        for e in range(start, stop):
            flat_along[4 * e : 4 * e + 4] = along[e]
        part = flat_along[4 * start : 4 * stop].astype(BF16)
        own_tiles[0][batch][b] = part if batch == 0 else part.reshape(2, 16, 128)
        send_batch(0, batch)

    arrived(plane.at[0:15], plane_recv.at[0])
    index = jnp.zeros((4, 128), F32)
    for dev in range(16):
        flat_rhs[4 * dev : 4 * dev + 4] = plane[dev, 0:4]
        flat_self[4 * dev : 4 * dev + 4] = plane[dev, 4:8]
        index += plane[dev, 8:12]
    squares = flat_rhs[...] * flat_rhs[...]
    send_sums(0, [total(squares), total(squares * flat_self[...])])
    index = index.astype(jnp.int32)
    spots = lax.broadcasted_iota(jnp.int32, (64, 256), 0) + 1
    selects = [
        jnp.where(
            spots == jnp.concatenate([index[2 * kind : 2 * kind + 1], index[2 * kind + 1 : 2 * kind + 2]], axis=1),
            1.0, 0.0,
        ).astype(BF16)
        for kind in range(2)
    ]

    def operate(it, before):
        finish_batch(it, 0)
        picks = picked(hot_first[it, 0], own_tiles[it][0][...])
        arrived(other_tiles[it][0], core_recv.at[it, 0])
        picks += picked(hot_first[it, 1], other_tiles[it][0][...])
        if it == 0:
            for load in loads[7:]:
                load.wait()
        send_terms(it, 0, near_terms(picks))
        pick[...] = picks
        finish_batch(it, 1)
        picks = pick[...] + picked(hot_middle[it, 0], own_tiles[it][1][...])
        arrived(other_tiles[it][1], core_recv.at[it, 1])
        picks += picked(hot_middle[it, 1], other_tiles[it][1][...])
        finish_batch(it, 2)
        picks += picked(hot_last[it], own_tiles[it][2][...])
        send_terms(it, 1, far_terms(picks))
        pair_sums(it)
        known = before(take_terms(it, 0, selects[0]))
        return known, take_terms(it, 1, selects[1])

    def before_1(sums_near):
        beta_squared, diagonal = take_sums(0, 2)
        beta = jnp.sqrt(beta_squared)
        guess = diagonal / beta_squared
        inverse = 1.0 / beta
        first = flat_rhs[...] * inverse
        image = (flat_self[...] * flat_rhs[...] + sums_near) * inverse
        return beta, guess, inverse, first, image, image - guess * first, total(first * first)

    (beta, guess, inverse, first, image, shifted, g11_here), sums_far = operate(0, before_1)
    sums_far = sums_far * inverse
    image = image + sums_far
    shifted = shifted + sums_far

    tile[...] = shifted.astype(BF16).reshape(4, 16, 128)

    even, quarter = x % 2, (y + 2 * (x // 2)) % 4

    def tile_copy(t, core=0):
        rank = 2 * t + (1 - even if t % 2 else even)
        away = (rank + 1) // 2
        d = away * (2 * (rank % 2) - 1)
        batch = (t + 2) // 4
        held = own_tiles[1][batch].at[0]
        part = held.at[t] if batch == 0 else held.at[t - 2] if batch == 1 else held.at[core, t - 6]
        recv = tile_recv.at[t if batch == 0 else batch + 1]
        return pltpu.make_async_remote_copy(
            src_ref=tile.at[quarter], dst_ref=part, send_sem=tile_send.at[int(t > 0)], recv_sem=recv,
            device_id=along_z(-d, 1 - c if core else c), device_id_type=MESH,
        )

    for t, core in ((7, 0), (7, 1), (6, 0), (6, 1), (5, 0), (4, 0), (3, 0), (2, 0), (1, 0)):
        tile_copy(t, core).start()
    sending(first_2.at[0, 0:4, 0], tile_send.at[1])
    sending(middle_2.at[0, 0, 0:4], tile_send.at[1])
    sending(first_2.at[0, 0, 0:1], tile_send.at[1])

    @pl.when(even > 0)
    def _():
        tile_copy(0).start()

    @pl.when(even == 0)
    def _():
        first_2[0, 0, 0] = tile[quarter]

    send_sums(1, [g11_here, total(first * shifted), total(shifted * shifted)])

    @pl.when(even > 0)
    def _():
        tile_copy(0).wait_recv()

    tile_copy(1).wait_recv()
    send_batch(1, 0)
    arrived(middle_2.at[0, 0], tile_recv.at[2])
    send_batch(1, 1)
    arrived(last_2.at[0], tile_recv.at[3])
    send_batch(1, 2)

    def before_2(sums_near):
        g11, p1, p2 = take_sums(1, 3)
        h11 = guess * g11 + p1
        step = h11 - guess
        h21 = jnp.sqrt(jnp.maximum(p2 - 2.0 * step * p1 + step * step * g11, 0.0) + 1e-06)
        inverse = 1.0 / h21
        basis = (shifted - step * first) * inverse
        rest = (flat_self[...] * shifted + sums_near - step * image) * inverse - guess * basis
        radius = jnp.sqrt(h11 * h11 + h21 * h21)
        return g11, h11, h21, inverse, basis, rest, radius, total(first * basis), total(basis * basis)

    (g11, h11, h21, inverse, basis, rest, radius, g12_here, g22_here), sums_far = operate(1, before_2)
    rest = rest + sums_far * inverse
    send_sums(2, [total(first * rest), total(basis * rest), total(rest * rest), g12_here, g22_here])

    def mine_of(value):
        flat_along[0:64] = value
        two = flat_along[pl.ds(pl.multiple_of((b // 2) * 8, 8), 8), :]
        return jnp.where(b % 2 == 0, two[:4], two[4:])

    own_first, own_basis, own_rest = mine_of(first), mine_of(basis), mine_of(rest)
    turn = 1.0 / radius
    cosine = h11 * turn
    sine = h21 * turn

    @pl.when(even > 0)
    def _():
        tile_copy(0).wait_send()

    settle()

    pair_sums(2)
    q1, q2, q3, g12, g22 = take_sums(2, 5)
    h12 = q1 + guess * g12
    h22 = q2 + guess * g22
    left_over = h22 - guess
    square = (
        q3 - 2.0 * h12 * q1 - 2.0 * left_over * q2
        + h12 * h12 * g11 + left_over * left_over * g22 + 2.0 * h12 * left_over * g12
    )
    square = jnp.maximum(square, 0.0) + 1e-06
    upper = cosine * h12 + sine * h22
    lower = cosine * h22 - sine * h12
    coef_two = -(lower / (lower * lower + square)) * (sine * beta)
    coef_one = (cosine * beta - upper * coef_two) * turn

    def wide(value):
        return jnp.concatenate([value[0:2], value[2:4]], axis=1)

    out[0] = wide(coef_one * own_first + coef_two * own_basis)
    out[1] = wide((own_rest - h12 * own_first - left_over * own_basis) * lax.rsqrt(square))

    settle()


def shards(rhs, self_term, near_blocks, near_row, near_col, far_left, far_right, far_row, far_col, far_rank):
    hbm = pl.BlockSpec(memory_space=pltpu.HBM)
    dma = pltpu.SemaphoreType.DMA
    out = pl.pallas_call(
        kernel,
        out_shape=jax.ShapeDtypeStruct((2, *rhs.shape), F32),
        in_specs=[hbm] * 10,
        out_specs=pl.BlockSpec(memory_space=pltpu.VMEM),
        scratch_shapes=[
            *[pltpu.SMEM(a.shape, jnp.int32) for a in (near_row, near_col, far_row, far_col, far_rank)],
            pltpu.VMEM(rhs.shape, F32), pltpu.VMEM(rhs.shape, F32),
            pltpu.VMEM(near_blocks.shape, BF16), pltpu.VMEM(far_left.shape, BF16), pltpu.VMEM(far_right.shape, BF16),
            dma((10,)),
            pltpu.VMEM((4, 128), F32), pltpu.VMEM((20, 4, 128), F32), dma((1,)), dma((3,)),
            pltpu.VMEM((16, 16, 128), F32), dma((1,)), dma((1,)),
            pltpu.VMEM((2, 16, 16, 128), BF16), pltpu.VMEM((2, 16, 2, 16, 128), BF16), pltpu.VMEM((16, 2, 16, 128), BF16),
            pltpu.VMEM((2, 8, 2, 16, 128), BF16), pltpu.VMEM((2, 8, 4, 16, 128), BF16),
            pltpu.VMEM((8, 2, 2, 16, 128), BF16), dma((2, 3)), dma((2, 3)), dma((2, 2)), dma((2, 2)),
            pltpu.VMEM((2, 2, 16, 16, 128), BF16), dma((2, 2)), dma((2, 2)),
            pltpu.VMEM((4, 16, 128), BF16), dma((2,)), dma((4,)),
            pltpu.VMEM((3, 23, 1, 128), F32), dma((3,)), dma((3, 2)),
            pltpu.VMEM((3, 2, 1, 128), F32), dma((3,)), dma((3,)),
            pltpu.VMEM((2, 2, 32, 256), BF16), pltpu.VMEM((2, 2, 32, 512), BF16), pltpu.VMEM((2, 32, 512), BF16),
            pltpu.VMEM((64, 128), F32), pltpu.VMEM((64, 128), F32), pltpu.VMEM((80, 128), F32),
            pltpu.VMEM((32, 128), F32),
        ],
        compiler_params=pltpu.CompilerParams(
            collective_id=0, has_side_effects=True, vmem_limit_bytes=56 * 1024 * 1024
        ),
        name="gmres",
    )(near_row, near_col, far_row, far_col, far_rank, rhs, self_term, near_blocks, far_left, far_right)
    return out[0], out[1]


def solution(mesh):
    vec = P(("rows", "bal"), None)
    blocks = P(("rows", "bal"), None, None)
    ints = P(("rows", "bal"))
    in_specs = (vec, vec, blocks, ints, ints, blocks, blocks, ints, ints, ints)
    return jax.shard_map(shards, mesh=mesh, in_specs=in_specs, out_specs=(vec, vec), check_vma=False)
```

```python
import jax
import jax.numpy as jnp
from jax import lax
from jax.experimental import pallas as pl
from jax.experimental.pallas import tpu as pltpu
from jax.sharding import PartitionSpec as P

MESH = pl.DeviceIdType.MESH
F32 = jnp.float32
BF16 = jnp.bfloat16
NEAR, FARS, RANK = 8, 6, 32

RING_HOPS = (0, 1, 2, 1)
PLANE = sorted(range(1, 16), key=lambda j: -(RING_HOPS[j // 4] + RING_HOPS[j % 4]))
ALONG = sorted(range(1, 16), key=lambda i: -min(i, 16 - i))


def signed(i):
    return i if i <= 8 else i - 16


def ranked(d):
    return 2 * abs(d) - (d > 0)


RANKS = {i: ranked(signed(-i % 16)) for i in ALONG}
OFFSETS = ((0, 0), (0, 1), (2, 0), (0, 3), (1, 0), (1, 1), (3, 0), (3, 1))
BOUNDS = ((0, 4, 3), (4, 12, 8), (12, 20, 8))


def total(value):
    return jnp.sum(jnp.sum(value, axis=0, keepdims=True), axis=1, keepdims=True)


def kernel(
    near_row_hbm, near_col_hbm, far_row_hbm, far_col_hbm, far_rank_hbm,
    rhs_hbm, self_hbm, near_hbm, left_hbm, right_hbm,
    out,
    near_row, near_col, far_row, far_col, far_rank, rhs, self_term,
    near, left, right, load_sem,
    own, along, along_send, along_recv,
    plane, plane_send, plane_recv,
    first_1, middle_1, last_1, first_2, middle_2, last_2, gather_send, gather_recv, core_send, core_recv,
    terms, terms_send, terms_recv,
    tile, tile_send, tile_recv,
    sums, sums_send, sums_recv, pair, pair_send, pair_recv,
    hot_first, hot_middle, hot_last, flat_rhs, flat_self, flat_along, pick,
):
    r = lax.axis_index("rows")
    b = lax.axis_index("bal")
    z, c = r // 2, r % 2
    x, y = b // 4, b % 4

    def along_z(i, core=c):
        return (((z + i + 16) % 16) * 2 + core, b)

    def in_plane(j):
        jx, jy = j // 4, j % 4
        px = x + jx - 2 * (x % 2) * (jx % 2) - 4 * ((x // 2) * (jx // 2))
        py = y + jy - 2 * (y % 2) * (jy % 2) - 4 * ((y // 2) * (jy // 2))
        return px * 4 + py

    sibling = (z * 2 + 1 - c, b)
    peer = {j: in_plane(j) for j in PLANE}
    both = [i for i in ALONG if RANKS[i] > 8]

    barrier = pltpu.get_barrier_semaphore()
    for i in ALONG:
        pl.semaphore_signal(barrier, inc=1, device_id=along_z(i), device_id_type=MESH)
    for i in both:
        pl.semaphore_signal(barrier, inc=1, device_id=along_z(i, 1 - c), device_id_type=MESH)
    for j in PLANE:
        pl.semaphore_signal(barrier, inc=1, device_id=(r, peer[j]), device_id_type=MESH)
    pl.semaphore_signal(barrier, inc=1, device_id=sibling, device_id_type=MESH)

    loads = [
        pltpu.make_async_copy(a, v, load_sem.at[n])
        for n, (a, v) in enumerate(
            (
                (rhs_hbm, rhs), (self_hbm, self_term), (near_row_hbm, near_row), (far_row_hbm, far_row),
                (near_col_hbm, near_col), (far_col_hbm, far_col), (far_rank_hbm, far_rank),
                (near_hbm, near), (left_hbm, left), (right_hbm, right),
            )
        )
    ]
    for load in loads:
        load.start()
    for load in loads[:7]:
        load.wait()

    def halves(value):
        return jnp.concatenate([value[:, :128], value[:, 128:]], axis=0)

    own_rhs = halves(rhs[...])
    own[...] = own_rhs
    along[0] = own_rhs

    base = r * 32
    lane = lax.broadcasted_iota(jnp.int32, (4, 128), 0) * 128 + lax.broadcasted_iota(jnp.int32, (4, 128), 1)
    mine = ((lane >> 4) & 15) == b
    half_of = (lane >> 3) & 1
    task_of = (lane & 7) + 8 * (lane >> 8)
    row_of = jnp.full((4, 128), -1, jnp.int32)
    for k in range(NEAR + FARS):
        local = (near_row[k] if k < NEAR else far_row[k - NEAR]) - base
        row_of = jnp.where(mine & (task_of == k), 2 * local - (local & 1), row_of)
    place = jnp.where(row_of >= 0, row_of + 2 * half_of + 1, 0).astype(F32)
    plane[b] = jnp.concatenate([own_rhs, halves(self_term[...]), place, jnp.zeros((4, 128), F32)], axis=0)

    pl.semaphore_wait(barrier, 31 + len(both))

    pending = []

    def send(src, dst, send_sem, recv_sem, device):
        pltpu.make_async_remote_copy(
            src_ref=src, dst_ref=dst, send_sem=send_sem, recv_sem=recv_sem, device_id=device, device_id_type=MESH
        ).start()

    def whole_stage(ref, send_sem, recv_sem):
        return pltpu.make_async_remote_copy(
            src_ref=ref, dst_ref=ref, send_sem=send_sem, recv_sem=recv_sem, device_id=sibling, device_id_type=MESH
        )

    def arrived(ref, recv_sem):
        whole_stage(ref, recv_sem, recv_sem).wait_recv()

    def sending(ref, send_sem):
        pending.append(whole_stage(ref, send_sem, send_sem))

    def settle():
        while pending:
            pending.pop().wait_send()

    for i in ALONG:
        rank = RANKS[i]
        batch = (rank // 4 + 1) // 2
        send(own, along.at[rank], along_send.at[0], along_recv.at[batch], along_z(i))
        if batch == 2:
            send(own, along.at[rank + 4], along_send.at[0], along_recv.at[batch], along_z(i, 1 - c))
    sending(along.at[0:19], along_send.at[0])
    for j in PLANE:
        send(plane.at[b], plane.at[b], plane_send.at[0], plane_recv.at[0], (r, peer[j]))
    sending(plane.at[0:15], plane_send.at[0])

    task = lax.broadcasted_iota(jnp.int32, (32, 1), 0)
    half = task >> 4
    place_1 = jnp.full((32, 1), -1, jnp.int32)
    place_2 = jnp.full((32, 1), -1, jnp.int32)
    for k in range(NEAR + FARS):
        col = near_col[k] if k < NEAR else far_col[k - NEAR]
        other = ((col >> 5) & 1) ^ c
        d = ((col >> 6) - z + 16) & 15
        dev = (col >> 1) & 15
        cl = col & 1
        rank = jnp.where(d == 0, 0, jnp.where(d <= 8, 2 * d - 1, 32 - 2 * d))
        tile_of, low = rank >> 2, rank & 3

        row = low * 4 + cl
        in_first = other * 256 + dev * 16 + row
        in_middle = 512 + other * 512 + dev * 32 + (tile_of - 1) * 16 + row
        in_last = 1536 + dev * 32 + other * 16 + row
        p1 = jnp.where(tile_of == 0, in_first, jnp.where(tile_of == 3, in_last, in_middle))
        t = rank >> 1
        away = ((rank ^ t) & 1) ^ (x % 2)
        slot = away * 4 + (((dev >> 2) - y - 2 * (((x + away) & 3) >> 1) + 8) & 3)
        row = (dev & 3) * 4 + cl
        in_first = ((other * 8 + slot) * 2 + t) * 16 + row
        in_middle = 512 + ((other * 8 + slot) * 4 + t - 2) * 16 + row
        in_last = 1536 + ((slot * 2 + other) * 2 + t - 6) * 16 + row
        p2 = jnp.where(t < 2, in_first, jnp.where(t >= 6, in_last, in_middle))
        place_1 = jnp.where((task & 15) == k, p1 + 2 * half, place_1)
        place_2 = jnp.where((task & 15) == k, p2 + 2 * half, place_2)
    spot = lax.broadcasted_iota(jnp.int32, (32, 512), 1)

    def hots(place, start, size):
        return jnp.where(spot[:, :size] + start == place, 1.0, 0.0).astype(BF16)

    for it, place in ((0, place_1), (1, place_2)):
        for other in range(2):
            hot_first[it, other] = hots(place, 256 * other, 256)
            hot_middle[it, other] = hots(place, 512 + 512 * other, 512)
        hot_last[it] = hots(place, 1536, 512)

    rank_of = jnp.zeros((16, 1), jnp.int32)
    task16 = lax.broadcasted_iota(jnp.int32, (16, 1), 0)
    for k in range(FARS):
        rank_of = jnp.where(task16 == NEAR + k, far_rank[k], rank_of)
    lane192 = lax.broadcasted_iota(jnp.int32, (16, FARS * RANK), 1)
    keep = ((lane192 >> 5) + NEAR == task16) & ((lane192 & 31) < rank_of)

    own_tiles = [[first_1.at[0], middle_1.at[0], last_1], [first_2.at[0], middle_2.at[0], last_2]]
    other_tiles = [[first_1.at[1], middle_1.at[1]], [first_2.at[1], middle_2.at[1]]]

    def send_batch(it, batch):
        held = own_tiles[it][batch]
        if it == 0:
            for j in PLANE:
                send(held.at[b], held.at[b], gather_send.at[it, batch], gather_recv.at[it, batch], (r, peer[j]))
            sending(held.at[0:15], gather_send.at[it, batch])
        else:
            for slot in (2, 5, 7, 1, 3, 4, 6):
                ox, oy = OFFSETS[slot]
                to = (r, ((x - ox + 4) % 4) * 4 + (y - oy + 4) % 4)
                send(held.at[0], held.at[slot], gather_send.at[it, batch], gather_recv.at[it, batch], to)
            sending(held.at[0:7], gather_send.at[it, batch])

    def finish_batch(it, batch):
        held = own_tiles[it][batch]
        arrived(held.at[0 : 7 if it else 15], gather_recv.at[it, batch])
        if batch < 2:
            send(held, other_tiles[it][batch], core_send.at[it, batch], core_recv.at[it, batch], sibling)
            sending(held, core_send.at[it, batch])

    def picked(hot, source):
        return jnp.dot(hot, source.reshape(-1, 128), preferred_element_type=F32)

    def joined(value):
        return jnp.concatenate([value[:16], value[16:]], axis=1)

    def send_terms(it, kind, value):
        terms[it, kind, b] = halves(value).astype(BF16)
        for j in PLANE:
            part = terms.at[it, kind, b]
            send(part, part, terms_send.at[it, kind], terms_recv.at[it, kind], (r, peer[j]))
        sending(terms.at[it, kind, 0:15], terms_send.at[it, kind])

    def take_terms(it, kind, select):
        arrived(terms.at[it, kind, 0:15], terms_recv.at[it, kind])
        return jnp.dot(select, terms[it, kind].reshape(256, 128), preferred_element_type=F32)

    def near_terms(picks):
        source = joined(picks)
        result = jnp.zeros((16, 256), F32)
        for k in range(NEAR):
            one = jnp.where(task16 == k, source, 0.0).astype(BF16)
            result += lax.dot_general(one, near[k], (((1,), (1,)), ((), ())), preferred_element_type=F32)
        return result[:8]

    def far_terms(picks):
        source = joined(picks).astype(BF16)
        coeff = lax.dot_general(
            source, right[...].reshape(FARS * RANK, 256), (((1,), (1,)), ((), ())), preferred_element_type=F32
        )
        coeff = jnp.where(keep, coeff, 0.0).astype(BF16)
        return jnp.dot(coeff, left[...].reshape(FARS * RANK, 256), preferred_element_type=F32)[8:]

    def send_sums(stage, values):
        lanes = lax.broadcasted_iota(jnp.int32, (1, 128), 1)
        row = jnp.zeros((1, 128), F32)
        for n, value in enumerate(values):
            row = jnp.where(lanes == n, value, row)
        sums[stage, 0] = row
        for i in ALONG:
            slot = RANKS[i]
            far = int(slot > 8)
            send(sums.at[stage, 0], sums.at[stage, slot], sums_send.at[stage], sums_recv.at[stage, far], along_z(i))
            if far and stage == 2:
                there = sums.at[stage, slot + 7]
                send(sums.at[stage, 0], there, sums_send.at[stage], sums_recv.at[stage, 1], along_z(i, 1 - c))
        sending(sums.at[stage, 0 : 22 if stage == 2 else 15], sums_send.at[stage])

    def pair_sums(stage):
        arrived(sums.at[stage, 0:8], sums_recv.at[stage, 0])
        if stage < 2:
            arrived(sums.at[stage, 0:7], sums_recv.at[stage, 1])
        pair[stage, 0] = jnp.sum(sums[stage, 0 : 9 if stage == 2 else 16], axis=0)
        send(pair.at[stage, 0], pair.at[stage, 1], pair_send.at[stage], pair_recv.at[stage], sibling)
        sending(pair.at[stage, 0], pair_send.at[stage])

    def take_sums(stage, count):
        arrived(pair.at[stage, 1], pair_recv.at[stage])
        row = pair[stage, 0] + pair[stage, 1]
        if stage == 2:
            arrived(sums.at[stage, 0:14], sums_recv.at[stage, 1])
            row += jnp.sum(sums[stage, 9:23], axis=0)
        return [row[:, n : n + 1] for n in range(count)]

    for batch, (start, stop, count) in enumerate(BOUNDS):
        arrived(along.at[0:count], along_recv.at[batch])
        for e in range(start, stop):
            flat_along[4 * e : 4 * e + 4] = along[e]
        part = flat_along[4 * start : 4 * stop].astype(BF16)
        own_tiles[0][batch][b] = part if batch == 0 else part.reshape(2, 16, 128)
        send_batch(0, batch)

    arrived(plane.at[0:15], plane_recv.at[0])
    index = jnp.zeros((4, 128), F32)
    for dev in range(16):
        flat_rhs[4 * dev : 4 * dev + 4] = plane[dev, 0:4]
        flat_self[4 * dev : 4 * dev + 4] = plane[dev, 4:8]
        index += plane[dev, 8:12]
    squares = flat_rhs[...] * flat_rhs[...]
    send_sums(0, [total(squares), total(squares * flat_self[...])])
    index = index.astype(jnp.int32)
    spots = lax.broadcasted_iota(jnp.int32, (64, 256), 0) + 1
    selects = [
        jnp.where(
            spots == jnp.concatenate([index[2 * kind : 2 * kind + 1], index[2 * kind + 1 : 2 * kind + 2]], axis=1),
            1.0, 0.0,
        ).astype(BF16)
        for kind in range(2)
    ]

    def operate(it, before):
        finish_batch(it, 0)
        picks = picked(hot_first[it, 0], own_tiles[it][0][...])
        arrived(other_tiles[it][0], core_recv.at[it, 0])
        picks += picked(hot_first[it, 1], other_tiles[it][0][...])
        if it == 0:
            for load in loads[7:]:
                load.wait()
        send_terms(it, 0, near_terms(picks))
        pick[...] = picks
        finish_batch(it, 1)
        picks = pick[...] + picked(hot_middle[it, 0], own_tiles[it][1][...])
        arrived(other_tiles[it][1], core_recv.at[it, 1])
        picks += picked(hot_middle[it, 1], other_tiles[it][1][...])
        finish_batch(it, 2)
        picks += picked(hot_last[it], own_tiles[it][2][...])
        send_terms(it, 1, far_terms(picks))
        pair_sums(it)
        known = before(take_terms(it, 0, selects[0]))
        return known, take_terms(it, 1, selects[1])

    def before_1(sums_near):
        beta_squared, diagonal = take_sums(0, 2)
        beta = jnp.sqrt(beta_squared)
        guess = diagonal / beta_squared
        inverse = 1.0 / beta
        first = flat_rhs[...] * inverse
        image = (flat_self[...] * flat_rhs[...] + sums_near) * inverse
        return beta, guess, inverse, first, image, image - guess * first, total(first * first)

    (beta, guess, inverse, first, image, shifted, g11_here), sums_far = operate(0, before_1)
    sums_far = sums_far * inverse
    image = image + sums_far
    shifted = shifted + sums_far

    tile[...] = shifted.astype(BF16).reshape(4, 16, 128)

    even, quarter = x % 2, (y + 2 * (x // 2)) % 4

    def tile_copy(t, core=0):
        rank = 2 * t + (1 - even if t % 2 else even)
        away = (rank + 1) // 2
        d = away * (2 * (rank % 2) - 1)
        batch = (t + 2) // 4
        held = own_tiles[1][batch].at[0]
        part = held.at[t] if batch == 0 else held.at[t - 2] if batch == 1 else held.at[core, t - 6]
        recv = tile_recv.at[t if batch == 0 else batch + 1]
        return pltpu.make_async_remote_copy(
            src_ref=tile.at[quarter], dst_ref=part, send_sem=tile_send.at[int(t > 0)], recv_sem=recv,
            device_id=along_z(-d, 1 - c if core else c), device_id_type=MESH,
        )

    for t, core in ((7, 0), (7, 1), (6, 0), (6, 1), (5, 0), (4, 0), (3, 0), (2, 0), (1, 0)):
        tile_copy(t, core).start()
    sending(first_2.at[0, 0:4, 0], tile_send.at[1])
    sending(middle_2.at[0, 0, 0:4], tile_send.at[1])
    sending(first_2.at[0, 0, 0:1], tile_send.at[1])

    @pl.when(even > 0)
    def _():
        tile_copy(0).start()

    @pl.when(even == 0)
    def _():
        first_2[0, 0, 0] = tile[quarter]

    send_sums(1, [g11_here, total(first * shifted), total(shifted * shifted)])

    @pl.when(even > 0)
    def _():
        tile_copy(0).wait_recv()

    tile_copy(1).wait_recv()
    send_batch(1, 0)
    arrived(middle_2.at[0, 0], tile_recv.at[2])
    send_batch(1, 1)
    arrived(last_2.at[0], tile_recv.at[3])
    send_batch(1, 2)

    def before_2(sums_near):
        g11, p1, p2 = take_sums(1, 3)
        h11 = guess * g11 + p1
        step = h11 - guess
        h21 = jnp.sqrt(jnp.maximum(p2 - 2.0 * step * p1 + step * step * g11, 0.0) + 1e-06)
        inverse = 1.0 / h21
        basis = (shifted - step * first) * inverse
        rest = (flat_self[...] * shifted + sums_near - step * image) * inverse - guess * basis
        radius = jnp.sqrt(h11 * h11 + h21 * h21)
        return g11, h11, h21, inverse, basis, rest, radius, total(first * basis), total(basis * basis)

    (g11, h11, h21, inverse, basis, rest, radius, g12_here, g22_here), sums_far = operate(1, before_2)
    rest = rest + sums_far * inverse
    send_sums(2, [total(first * rest), total(basis * rest), total(rest * rest), g12_here, g22_here])

    def mine_of(value):
        flat_along[0:64] = value
        two = flat_along[pl.ds(pl.multiple_of((b // 2) * 8, 8), 8), :]
        return jnp.where(b % 2 == 0, two[:4], two[4:])

    own_first, own_basis, own_rest = mine_of(first), mine_of(basis), mine_of(rest)
    turn = 1.0 / radius
    cosine = h11 * turn
    sine = h21 * turn

    @pl.when(even > 0)
    def _():
        tile_copy(0).wait_send()

    settle()

    pair_sums(2)
    q1, q2, q3, g12, g22 = take_sums(2, 5)
    h12 = q1 + guess * g12
    h22 = q2 + guess * g22
    left_over = h22 - guess
    square = (
        q3 - 2.0 * h12 * q1 - 2.0 * left_over * q2
        + h12 * h12 * g11 + left_over * left_over * g22 + 2.0 * h12 * left_over * g12
    )
    square = jnp.maximum(square, 0.0) + 1e-06
    upper = cosine * h12 + sine * h22
    lower = cosine * h22 - sine * h12
    coef_two = -(lower / (lower * lower + square)) * (sine * beta)
    coef_one = (cosine * beta - upper * coef_two) * turn

    def wide(value):
        return jnp.concatenate([value[0:2], value[2:4]], axis=1)

    out[0] = wide(coef_one * own_first + coef_two * own_basis)
    out[1] = wide((own_rest - h12 * own_first - left_over * own_basis) * lax.rsqrt(square))

    settle()


def shards(rhs, self_term, near_blocks, near_row, near_col, far_left, far_right, far_row, far_col, far_rank):
    hbm = pl.BlockSpec(memory_space=pltpu.HBM)
    dma = pltpu.SemaphoreType.DMA
    out = pl.pallas_call(
        kernel,
        out_shape=pltpu.VMEM((2, *rhs.shape), F32),
        in_specs=[hbm] * 10,
        out_specs=pl.BlockSpec(memory_space=pltpu.VMEM),
        scratch_shapes=[
            *[pltpu.SMEM(a.shape, jnp.int32) for a in (near_row, near_col, far_row, far_col, far_rank)],
            pltpu.VMEM(rhs.shape, F32), pltpu.VMEM(rhs.shape, F32),
            pltpu.VMEM(near_blocks.shape, BF16), pltpu.VMEM(far_left.shape, BF16), pltpu.VMEM(far_right.shape, BF16),
            dma((10,)),
            pltpu.VMEM((4, 128), F32), pltpu.VMEM((20, 4, 128), F32), dma((1,)), dma((3,)),
            pltpu.VMEM((16, 16, 128), F32), dma((1,)), dma((1,)),
            pltpu.VMEM((2, 16, 16, 128), BF16), pltpu.VMEM((2, 16, 2, 16, 128), BF16), pltpu.VMEM((16, 2, 16, 128), BF16),
            pltpu.VMEM((2, 8, 2, 16, 128), BF16), pltpu.VMEM((2, 8, 4, 16, 128), BF16),
            pltpu.VMEM((8, 2, 2, 16, 128), BF16), dma((2, 3)), dma((2, 3)), dma((2, 2)), dma((2, 2)),
            pltpu.VMEM((2, 2, 16, 16, 128), BF16), dma((2, 2)), dma((2, 2)),
            pltpu.VMEM((4, 16, 128), BF16), dma((2,)), dma((4,)),
            pltpu.VMEM((3, 23, 1, 128), F32), dma((3,)), dma((3, 2)),
            pltpu.VMEM((3, 2, 1, 128), F32), dma((3,)), dma((3,)),
            pltpu.VMEM((2, 2, 32, 256), BF16), pltpu.VMEM((2, 2, 32, 512), BF16), pltpu.VMEM((2, 32, 512), BF16),
            pltpu.VMEM((64, 128), F32), pltpu.VMEM((64, 128), F32), pltpu.VMEM((80, 128), F32),
            pltpu.VMEM((32, 128), F32),
        ],
        compiler_params=pltpu.CompilerParams(
            collective_id=0, has_side_effects=True, vmem_limit_bytes=56 * 1024 * 1024
        ),
        name="gmres",
    )(near_row, near_col, far_row, far_col, far_rank, rhs, self_term, near_blocks, far_left, far_right)
    return out[0], out[1]


def solution(mesh):
    vec = P(("rows", "bal"), None)
    blocks = P(("rows", "bal"), None, None)
    ints = P(("rows", "bal"))
    in_specs = (vec, vec, blocks, ints, ints, blocks, blocks, ints, ints, ints)
    return jax.shard_map(shards, mesh=mesh, in_specs=in_specs, out_specs=(vec, vec), check_vma=False)
```

```python
import jax
import jax.numpy as jnp
from jax import lax
from jax.experimental import pallas as pl
from jax.experimental.pallas import tpu as pltpu
from jax.sharding import PartitionSpec as P

MESH = pl.DeviceIdType.MESH
F32 = jnp.float32
BF16 = jnp.bfloat16
NEAR, FARS, RANK = 8, 6, 32

RING_HOPS = (0, 1, 2, 1)
PLANE = sorted(range(1, 16), key=lambda j: -(RING_HOPS[j // 4] + RING_HOPS[j % 4]))
ALONG = sorted(range(1, 16), key=lambda i: -min(i, 16 - i))


def signed(i):
    return i if i <= 8 else i - 16


def ranked(d):
    return 2 * abs(d) - (d > 0)


RANKS = {i: ranked(signed(-i % 16)) for i in ALONG}
OFFSETS = ((0, 0), (0, 1), (0, 2), (0, 3), (1, 0), (3, 3), (3, 0), (1, 3))
BOUNDS = ((0, 4, 3), (4, 12, 8), (12, 20, 8))


def total(value):
    return jnp.sum(jnp.sum(value, axis=0, keepdims=True), axis=1, keepdims=True)


def kernel(
    near_row_hbm, near_col_hbm, far_row_hbm, far_col_hbm, far_rank_hbm,
    rhs_hbm, self_hbm, near_hbm, left_hbm, right_hbm,
    out,
    near_row, near_col, far_row, far_col, far_rank, rhs, self_term,
    near, left, right, load_sem,
    own, along, along_send, along_recv,
    plane, plane_send, plane_recv,
    first_1, middle_1, last_1, first_2, middle_2, last_2, gather_send, gather_recv, core_send, core_recv,
    terms, terms_send, terms_recv,
    tile, tile_send, tile_recv,
    sums, sums_send, sums_recv, pair, pair_send, pair_recv,
    hot_first, hot_middle, hot_last, flat_rhs, flat_self, flat_along, pick,
):
    r = lax.axis_index("rows")
    b = lax.axis_index("bal")
    z, c = r // 2, r % 2
    x, y = b // 4, b % 4

    def along_z(i, core=c):
        return (((z + i + 16) % 16) * 2 + core, b)

    def in_plane(j):
        jx, jy = j // 4, j % 4
        px = x + jx - 2 * (x % 2) * (jx % 2) - 4 * ((x // 2) * (jx // 2))
        py = y + jy - 2 * (y % 2) * (jy % 2) - 4 * ((y // 2) * (jy // 2))
        return px * 4 + py

    sibling = (z * 2 + 1 - c, b)
    peer = {j: in_plane(j) for j in PLANE}
    both = [i for i in ALONG if RANKS[i] > 8]

    barrier = pltpu.get_barrier_semaphore()
    for i in ALONG:
        pl.semaphore_signal(barrier, inc=1, device_id=along_z(i), device_id_type=MESH)
    for i in both:
        pl.semaphore_signal(barrier, inc=1, device_id=along_z(i, 1 - c), device_id_type=MESH)
    for j in PLANE:
        pl.semaphore_signal(barrier, inc=1, device_id=(r, peer[j]), device_id_type=MESH)
    pl.semaphore_signal(barrier, inc=1, device_id=sibling, device_id_type=MESH)

    loads = [
        pltpu.make_async_copy(a, v, load_sem.at[n])
        for n, (a, v) in enumerate(
            (
                (rhs_hbm, rhs), (self_hbm, self_term), (near_row_hbm, near_row), (far_row_hbm, far_row),
                (near_col_hbm, near_col), (far_col_hbm, far_col), (far_rank_hbm, far_rank),
                (near_hbm, near), (left_hbm, left), (right_hbm, right),
            )
        )
    ]
    for load in loads:
        load.start()
    for load in loads[:7]:
        load.wait()

    def halves(value):
        return jnp.concatenate([value[:, :128], value[:, 128:]], axis=0)

    own_rhs = halves(rhs[...])
    own[...] = own_rhs
    along[0] = own_rhs

    base = r * 32
    lane = lax.broadcasted_iota(jnp.int32, (4, 128), 0) * 128 + lax.broadcasted_iota(jnp.int32, (4, 128), 1)
    mine = ((lane >> 4) & 15) == b
    half_of = (lane >> 3) & 1
    task_of = (lane & 7) + 8 * (lane >> 8)
    row_of = jnp.full((4, 128), -1, jnp.int32)
    for k in range(NEAR + FARS):
        local = (near_row[k] if k < NEAR else far_row[k - NEAR]) - base
        row_of = jnp.where(mine & (task_of == k), 2 * local - (local & 1), row_of)
    place = jnp.where(row_of >= 0, row_of + 2 * half_of + 1, 0).astype(F32)
    plane[b] = jnp.concatenate([own_rhs, halves(self_term[...]), place, jnp.zeros((4, 128), F32)], axis=0)

    pl.semaphore_wait(barrier, 31 + len(both))

    pending = []

    def send(src, dst, send_sem, recv_sem, device):
        pltpu.make_async_remote_copy(
            src_ref=src, dst_ref=dst, send_sem=send_sem, recv_sem=recv_sem, device_id=device, device_id_type=MESH
        ).start()

    def whole_stage(ref, send_sem, recv_sem):
        return pltpu.make_async_remote_copy(
            src_ref=ref, dst_ref=ref, send_sem=send_sem, recv_sem=recv_sem, device_id=sibling, device_id_type=MESH
        )

    def arrived(ref, recv_sem):
        whole_stage(ref, recv_sem, recv_sem).wait_recv()

    def sending(ref, send_sem):
        pending.append(whole_stage(ref, send_sem, send_sem))

    def settle():
        while pending:
            pending.pop().wait_send()

    for i in ALONG:
        rank = RANKS[i]
        batch = (rank // 4 + 1) // 2
        send(own, along.at[rank], along_send.at[0], along_recv.at[batch], along_z(i))
        if batch == 2:
            send(own, along.at[rank + 4], along_send.at[0], along_recv.at[batch], along_z(i, 1 - c))
    sending(along.at[0:19], along_send.at[0])
    for j in PLANE:
        send(plane.at[b], plane.at[b], plane_send.at[0], plane_recv.at[0], (r, peer[j]))
    sending(plane.at[0:15], plane_send.at[0])

    task = lax.broadcasted_iota(jnp.int32, (32, 1), 0)
    half = task >> 4
    place_1 = jnp.full((32, 1), -1, jnp.int32)
    place_2 = jnp.full((32, 1), -1, jnp.int32)
    for k in range(NEAR + FARS):
        col = near_col[k] if k < NEAR else far_col[k - NEAR]
        other = ((col >> 5) & 1) ^ c
        d = ((col >> 6) - z + 16) & 15
        dev = (col >> 1) & 15
        cl = col & 1
        rank = jnp.where(d == 0, 0, jnp.where(d <= 8, 2 * d - 1, 32 - 2 * d))
        tile_of, low = rank >> 2, rank & 3

        row = low * 4 + cl
        in_first = other * 256 + dev * 16 + row
        in_middle = 512 + other * 512 + dev * 32 + (tile_of - 1) * 16 + row
        in_last = 1536 + dev * 32 + other * 16 + row
        p1 = jnp.where(tile_of == 0, in_first, jnp.where(tile_of == 3, in_last, in_middle))
        t = rank >> 1
        away = ((rank ^ t) & 1) ^ (x % 2)
        slot = away * 4 + (((dev >> 2) - y - 2 * (((x + away) & 3) >> 1) + 8) & 3)
        row = (dev & 3) * 4 + cl
        in_first = ((other * 8 + slot) * 2 + t) * 16 + row
        in_middle = 512 + ((other * 8 + slot) * 4 + t - 2) * 16 + row
        in_last = 1536 + ((slot * 2 + other) * 2 + t - 6) * 16 + row
        p2 = jnp.where(t < 2, in_first, jnp.where(t >= 6, in_last, in_middle))
        place_1 = jnp.where((task & 15) == k, p1 + 2 * half, place_1)
        place_2 = jnp.where((task & 15) == k, p2 + 2 * half, place_2)
    spot = lax.broadcasted_iota(jnp.int32, (32, 512), 1)

    def hots(place, start, size):
        return jnp.where(spot[:, :size] + start == place, 1.0, 0.0).astype(BF16)

    for it, place in ((0, place_1), (1, place_2)):
        for other in range(2):
            hot_first[it, other] = hots(place, 256 * other, 256)
            hot_middle[it, other] = hots(place, 512 + 512 * other, 512)
        hot_last[it] = hots(place, 1536, 512)

    rank_of = jnp.zeros((16, 1), jnp.int32)
    task16 = lax.broadcasted_iota(jnp.int32, (16, 1), 0)
    for k in range(FARS):
        rank_of = jnp.where(task16 == NEAR + k, far_rank[k], rank_of)
    lane192 = lax.broadcasted_iota(jnp.int32, (16, FARS * RANK), 1)
    keep = ((lane192 >> 5) + NEAR == task16) & ((lane192 & 31) < rank_of)

    own_tiles = [[first_1.at[0], middle_1.at[0], last_1], [first_2.at[0], middle_2.at[0], last_2]]
    other_tiles = [[first_1.at[1], middle_1.at[1]], [first_2.at[1], middle_2.at[1]]]

    def send_batch(it, batch):
        held = own_tiles[it][batch]
        if it == 0:
            for j in PLANE:
                send(held.at[b], held.at[b], gather_send.at[it, batch], gather_recv.at[it, batch], (r, peer[j]))
            sending(held.at[0:15], gather_send.at[it, batch])
        else:
            for slot in (2, 5, 7, 1, 3, 4, 6):
                ox, oy = OFFSETS[slot]
                to = (r, ((x - ox + 4) % 4) * 4 + (y - oy + 4) % 4)
                send(held.at[0], held.at[slot], gather_send.at[it, batch], gather_recv.at[it, batch], to)
            sending(held.at[0:7], gather_send.at[it, batch])

    def finish_batch(it, batch):
        held = own_tiles[it][batch]
        arrived(held.at[0 : 7 if it else 15], gather_recv.at[it, batch])
        if batch < 2:
            send(held, other_tiles[it][batch], core_send.at[it, batch], core_recv.at[it, batch], sibling)
            sending(held, core_send.at[it, batch])

    def picked(hot, source):
        return jnp.dot(hot, source.reshape(-1, 128), preferred_element_type=F32)

    def joined(value):
        return jnp.concatenate([value[:16], value[16:]], axis=1)

    def send_terms(it, kind, value):
        terms[it, kind, b] = halves(value).astype(BF16)
        for j in PLANE:
            part = terms.at[it, kind, b]
            send(part, part, terms_send.at[it, kind], terms_recv.at[it, kind], (r, peer[j]))
        sending(terms.at[it, kind, 0:15], terms_send.at[it, kind])

    def take_terms(it, kind, select):
        arrived(terms.at[it, kind, 0:15], terms_recv.at[it, kind])
        return jnp.dot(select, terms[it, kind].reshape(256, 128), preferred_element_type=F32)

    def near_terms(picks):
        source = joined(picks)
        result = jnp.zeros((16, 256), F32)
        for k in range(NEAR):
            one = jnp.where(task16 == k, source, 0.0).astype(BF16)
            result += lax.dot_general(one, near[k], (((1,), (1,)), ((), ())), preferred_element_type=F32)
        return result[:8]

    def far_terms(picks):
        source = joined(picks).astype(BF16)
        coeff = lax.dot_general(
            source, right[...].reshape(FARS * RANK, 256), (((1,), (1,)), ((), ())), preferred_element_type=F32
        )
        coeff = jnp.where(keep, coeff, 0.0).astype(BF16)
        return jnp.dot(coeff, left[...].reshape(FARS * RANK, 256), preferred_element_type=F32)[8:]

    def send_sums(stage, values):
        lanes = lax.broadcasted_iota(jnp.int32, (1, 128), 1)
        row = jnp.zeros((1, 128), F32)
        for n, value in enumerate(values):
            row = jnp.where(lanes == n, value, row)
        sums[stage, 0] = row
        for i in ALONG:
            slot = RANKS[i]
            far = int(slot > 8)
            send(sums.at[stage, 0], sums.at[stage, slot], sums_send.at[stage], sums_recv.at[stage, far], along_z(i))
            if far and stage == 2:
                there = sums.at[stage, slot + 7]
                send(sums.at[stage, 0], there, sums_send.at[stage], sums_recv.at[stage, 1], along_z(i, 1 - c))
        sending(sums.at[stage, 0 : 22 if stage == 2 else 15], sums_send.at[stage])

    def pair_sums(stage):
        arrived(sums.at[stage, 0:8], sums_recv.at[stage, 0])
        if stage < 2:
            arrived(sums.at[stage, 0:7], sums_recv.at[stage, 1])
        pair[stage, 0] = jnp.sum(sums[stage, 0 : 9 if stage == 2 else 16], axis=0)
        send(pair.at[stage, 0], pair.at[stage, 1], pair_send.at[stage], pair_recv.at[stage], sibling)
        sending(pair.at[stage, 0], pair_send.at[stage])

    def spread(value):
        return jnp.broadcast_to(value, (4, 128))

    def take_sums(stage, count):
        arrived(pair.at[stage, 1], pair_recv.at[stage])
        row = pair[stage, 0] + pair[stage, 1]
        if stage == 2:
            arrived(sums.at[stage, 0:14], sums_recv.at[stage, 1])
            row += jnp.sum(sums[stage, 9:23], axis=0)
        return [spread(row[:, n : n + 1]) if stage == 2 else row[:, n : n + 1] for n in range(count)]

    def along_batch(batch):
        start, stop, count = BOUNDS[batch]
        arrived(along.at[0:count], along_recv.at[batch])
        for e in range(start, stop):
            flat_along[4 * e : 4 * e + 4] = along[e]
        part = flat_along[4 * start : 4 * stop].astype(BF16)
        own_tiles[0][batch][b] = part if batch == 0 else part.reshape(2, 16, 128)
        send_batch(0, batch)

    along_batch(0)
    arrived(plane.at[0:15], plane_recv.at[0])
    index = jnp.zeros((4, 128), F32)
    for dev in range(16):
        flat_rhs[4 * dev : 4 * dev + 4] = plane[dev, 0:4]
        flat_self[4 * dev : 4 * dev + 4] = plane[dev, 4:8]
        index += plane[dev, 8:12]
    squares = flat_rhs[...] * flat_rhs[...]
    squares_here, diagonal_here = total(squares), total(squares * flat_self[...])
    along_batch(1)
    along_batch(2)
    send_sums(0, [squares_here, diagonal_here])
    index = index.astype(jnp.int32)
    spots = lax.broadcasted_iota(jnp.int32, (64, 256), 0) + 1
    selects = [
        jnp.where(
            spots == jnp.concatenate([index[2 * kind : 2 * kind + 1], index[2 * kind + 1 : 2 * kind + 2]], axis=1),
            1.0, 0.0,
        ).astype(BF16)
        for kind in range(2)
    ]

    def operate(it, before):
        finish_batch(it, 0)
        picks = picked(hot_first[it, 0], own_tiles[it][0][...])
        arrived(other_tiles[it][0], core_recv.at[it, 0])
        picks += picked(hot_first[it, 1], other_tiles[it][0][...])
        if it == 0:
            for load in loads[7:]:
                load.wait()
        send_terms(it, 0, near_terms(picks))
        pick[...] = picks
        finish_batch(it, 1)
        picks = pick[...] + picked(hot_middle[it, 0], own_tiles[it][1][...])
        arrived(other_tiles[it][1], core_recv.at[it, 1])
        picks += picked(hot_middle[it, 1], other_tiles[it][1][...])
        finish_batch(it, 2)
        picks += picked(hot_last[it], own_tiles[it][2][...])
        send_terms(it, 1, far_terms(picks))
        pair_sums(it)
        known = before(take_terms(it, 0, selects[0]))
        return known, take_terms(it, 1, selects[1])

    def before_1(sums_near):
        beta_squared, diagonal = take_sums(0, 2)
        beta = jnp.sqrt(beta_squared)
        guess = diagonal / beta_squared
        inverse = 1.0 / beta
        first = flat_rhs[...] * inverse
        image = (flat_self[...] * flat_rhs[...] + sums_near) * inverse
        return beta, guess, inverse, first, image, image - guess * first, total(first * first)

    (beta, guess, inverse, first, image, shifted, g11_here), sums_far = operate(0, before_1)
    sums_far = sums_far * inverse
    image = image + sums_far
    shifted = shifted + sums_far

    tile[...] = shifted.astype(BF16).reshape(4, 16, 128)

    even, quarter = x % 2, (y + 2 * (x // 2)) % 4

    def tile_copy(t, core=0):
        rank = 2 * t + (1 - even if t % 2 else even)
        away = (rank + 1) // 2
        d = away * (2 * (rank % 2) - 1)
        batch = (t + 2) // 4
        held = own_tiles[1][batch].at[0]
        part = held.at[t] if batch == 0 else held.at[t - 2] if batch == 1 else held.at[core, t - 6]
        recv = tile_recv.at[t if batch == 0 else batch + 1]
        return pltpu.make_async_remote_copy(
            src_ref=tile.at[quarter], dst_ref=part, send_sem=tile_send.at[int(t > 0)], recv_sem=recv,
            device_id=along_z(-d, 1 - c if core else c), device_id_type=MESH,
        )

    for t, core in ((7, 0), (7, 1), (6, 0), (6, 1), (5, 0), (4, 0), (3, 0), (2, 0), (1, 0)):
        tile_copy(t, core).start()
    sending(first_2.at[0, 0:4, 0], tile_send.at[1])
    sending(middle_2.at[0, 0, 0:4], tile_send.at[1])
    sending(first_2.at[0, 0, 0:1], tile_send.at[1])

    @pl.when(even > 0)
    def _():
        tile_copy(0).start()

    @pl.when(even == 0)
    def _():
        first_2[0, 0, 0] = tile[quarter]

    send_sums(1, [g11_here, total(first * shifted), total(shifted * shifted)])

    @pl.when(even > 0)
    def _():
        tile_copy(0).wait_recv()

    tile_copy(1).wait_recv()
    send_batch(1, 0)
    arrived(middle_2.at[0, 0], tile_recv.at[2])
    send_batch(1, 1)
    arrived(last_2.at[0], tile_recv.at[3])
    send_batch(1, 2)

    def before_2(sums_near):
        g11, p1, p2 = take_sums(1, 3)
        h11 = guess * g11 + p1
        step = h11 - guess
        h21 = jnp.sqrt(jnp.maximum(p2 - 2.0 * step * p1 + step * step * g11, 0.0) + 1e-06)
        inverse = 1.0 / h21
        basis = (shifted - step * first) * inverse
        rest = (flat_self[...] * shifted + sums_near - step * image) * inverse - guess * basis
        radius = jnp.sqrt(h11 * h11 + h21 * h21)
        return g11, h11, h21, inverse, basis, rest, radius, total(first * basis), total(basis * basis)

    (g11, h11, h21, inverse, basis, rest, radius, g12_here, g22_here), sums_far = operate(1, before_2)
    rest = rest + sums_far * inverse
    send_sums(2, [total(first * rest), total(basis * rest), total(rest * rest), g12_here, g22_here])

    def mine_of(value):
        flat_along[0:64] = value
        two = flat_along[pl.ds(pl.multiple_of((b // 2) * 8, 8), 8), :]
        return jnp.where(b % 2 == 0, two[:4], two[4:])

    own_first, own_basis, own_rest = mine_of(first), mine_of(basis), mine_of(rest)
    turn = 1.0 / radius
    cosine, sine, sine_beta, cosine_beta = h11 * turn, h21 * turn, h21 * turn * beta, h11 * turn * beta
    turn, cosine, sine, sine_beta, cosine_beta = map(spread, (turn, cosine, sine, sine_beta, cosine_beta))
    guess, g11 = spread(guess), spread(g11)

    @pl.when(even > 0)
    def _():
        tile_copy(0).wait_send()

    settle()

    pair_sums(2)
    q1, q2, q3, g12, g22 = take_sums(2, 5)
    h12 = q1 + guess * g12
    h22 = q2 + guess * g22
    left_over = h22 - guess
    square = (
        q3 - 2.0 * h12 * q1 - 2.0 * left_over * q2
        + h12 * h12 * g11 + left_over * left_over * g22 + 2.0 * h12 * left_over * g12
    )
    square = jnp.maximum(square, 0.0) + 1e-06
    upper = cosine * h12 + sine * h22
    lower = cosine * h22 - sine * h12
    coef_two = -(lower / (lower * lower + square)) * sine_beta
    coef_one = (cosine_beta - upper * coef_two) * turn

    def wide(value):
        return jnp.concatenate([value[0:2], value[2:4]], axis=1)

    out[0] = wide(coef_one * own_first + coef_two * own_basis)
    out[1] = wide((own_rest - h12 * own_first - left_over * own_basis) * lax.rsqrt(square))

    settle()


def shards(rhs, self_term, near_blocks, near_row, near_col, far_left, far_right, far_row, far_col, far_rank):
    hbm = pl.BlockSpec(memory_space=pltpu.HBM)
    dma = pltpu.SemaphoreType.DMA
    out = pl.pallas_call(
        kernel,
        out_shape=pltpu.VMEM((2, *rhs.shape), F32),
        in_specs=[hbm] * 10,
        out_specs=pl.BlockSpec(memory_space=pltpu.VMEM),
        scratch_shapes=[
            *[pltpu.SMEM(a.shape, jnp.int32) for a in (near_row, near_col, far_row, far_col, far_rank)],
            pltpu.VMEM(rhs.shape, F32), pltpu.VMEM(rhs.shape, F32),
            pltpu.VMEM(near_blocks.shape, BF16), pltpu.VMEM(far_left.shape, BF16), pltpu.VMEM(far_right.shape, BF16),
            dma((10,)),
            pltpu.VMEM((4, 128), F32), pltpu.VMEM((20, 4, 128), F32), dma((1,)), dma((3,)),
            pltpu.VMEM((16, 16, 128), F32), dma((1,)), dma((1,)),
            pltpu.VMEM((2, 16, 16, 128), BF16), pltpu.VMEM((2, 16, 2, 16, 128), BF16), pltpu.VMEM((16, 2, 16, 128), BF16),
            pltpu.VMEM((2, 8, 2, 16, 128), BF16), pltpu.VMEM((2, 8, 4, 16, 128), BF16),
            pltpu.VMEM((8, 2, 2, 16, 128), BF16), dma((2, 3)), dma((2, 3)), dma((2, 2)), dma((2, 2)),
            pltpu.VMEM((2, 2, 16, 16, 128), BF16), dma((2, 2)), dma((2, 2)),
            pltpu.VMEM((4, 16, 128), BF16), dma((2,)), dma((4,)),
            pltpu.VMEM((3, 23, 1, 128), F32), dma((3,)), dma((3, 2)),
            pltpu.VMEM((3, 2, 1, 128), F32), dma((3,)), dma((3,)),
            pltpu.VMEM((2, 2, 32, 256), BF16), pltpu.VMEM((2, 2, 32, 512), BF16), pltpu.VMEM((2, 32, 512), BF16),
            pltpu.VMEM((64, 128), F32), pltpu.VMEM((64, 128), F32), pltpu.VMEM((80, 128), F32),
            pltpu.VMEM((32, 128), F32),
        ],
        compiler_params=pltpu.CompilerParams(
            collective_id=0, has_side_effects=True, vmem_limit_bytes=56 * 1024 * 1024
        ),
        name="gmres",
    )(near_row, near_col, far_row, far_col, far_rank, rhs, self_term, near_blocks, far_left, far_right)
    return out[0], out[1]


def solution(mesh):
    vec = P(("rows", "bal"), None)
    blocks = P(("rows", "bal"), None, None)
    ints = P(("rows", "bal"))
    in_specs = (vec, vec, blocks, ints, ints, blocks, blocks, ints, ints, ints)
    return jax.shard_map(shards, mesh=mesh, in_specs=in_specs, out_specs=(vec, vec), check_vma=False)
```

```python
import jax
import jax.numpy as jnp
from jax import lax
from jax.experimental import pallas as pl
from jax.experimental.pallas import tpu as pltpu
from jax.sharding import PartitionSpec as P

MESH = pl.DeviceIdType.MESH
F32 = jnp.float32
BF16 = jnp.bfloat16
NEAR, FARS, RANK = 8, 6, 32

RING_HOPS = (0, 1, 2, 1)
PLANE = sorted(range(1, 16), key=lambda j: -(RING_HOPS[j // 4] + RING_HOPS[j % 4]))
ALONG = sorted(range(1, 16), key=lambda i: -min(i, 16 - i))


def signed(i):
    return i if i <= 8 else i - 16


def ranked(d):
    return 2 * abs(d) - (d > 0)


RANKS = {i: ranked(signed(-i % 16)) for i in ALONG}
OFFSETS = ((0, 0), (0, 1), (0, 2), (0, 3), (1, 0), (3, 3), (3, 0), (1, 3))
BOUNDS = ((0, 4, 3), (4, 12, 8), (12, 20, 8))


def total(value):
    return jnp.sum(jnp.sum(value, axis=0, keepdims=True), axis=1, keepdims=True)


def kernel(
    near_row_hbm, near_col_hbm, far_row_hbm, far_col_hbm, far_rank_hbm,
    rhs_hbm, self_hbm, near_hbm, left_hbm, right_hbm,
    out,
    near_row, near_col, far_row, far_col, far_rank, rhs, self_term,
    near, left, right, load_sem,
    own, along, along_send, along_recv,
    plane, plane_send, plane_recv,
    first_1, middle_1, last_1, first_2, middle_2, last_2, gather_send, gather_recv, core_send, core_recv,
    terms, terms_send, terms_recv,
    tile, tile_send, tile_recv,
    sums, sums_send, sums_recv, pair, pair_send, pair_recv,
    hot_first, hot_middle, hot_last, flat_rhs, flat_self, flat_along, pick,
):
    r = lax.axis_index("rows")
    b = lax.axis_index("bal")
    z, c = r // 2, r % 2
    x, y = b // 4, b % 4

    def along_z(i, core=c):
        return (((z + i + 16) % 16) * 2 + core, b)

    def in_plane(j):
        jx, jy = j // 4, j % 4
        px = x + jx - 2 * (x % 2) * (jx % 2) - 4 * ((x // 2) * (jx // 2))
        py = y + jy - 2 * (y % 2) * (jy % 2) - 4 * ((y // 2) * (jy // 2))
        return px * 4 + py

    sibling = (z * 2 + 1 - c, b)
    peer = {j: in_plane(j) for j in PLANE}
    both = [i for i in ALONG if RANKS[i] > 8]

    barrier = pltpu.get_barrier_semaphore()
    for i in ALONG:
        pl.semaphore_signal(barrier, inc=1, device_id=along_z(i), device_id_type=MESH)
    for i in both:
        pl.semaphore_signal(barrier, inc=1, device_id=along_z(i, 1 - c), device_id_type=MESH)
    for j in PLANE:
        pl.semaphore_signal(barrier, inc=1, device_id=(r, peer[j]), device_id_type=MESH)
    pl.semaphore_signal(barrier, inc=1, device_id=sibling, device_id_type=MESH)

    loads = [
        pltpu.make_async_copy(a, v, load_sem.at[n])
        for n, (a, v) in enumerate(
            (
                (rhs_hbm, rhs), (self_hbm, self_term), (near_row_hbm, near_row), (far_row_hbm, far_row),
                (near_col_hbm, near_col), (far_col_hbm, far_col), (far_rank_hbm, far_rank),
                (near_hbm, near), (left_hbm, left), (right_hbm, right),
            )
        )
    ]
    for load in loads:
        load.start()
    for load in loads[:7]:
        load.wait()

    def halves(value):
        return jnp.concatenate([value[:, :128], value[:, 128:]], axis=0)

    own_rhs = halves(rhs[...])
    own[...] = own_rhs
    along[0] = own_rhs

    base = r * 32
    lane = lax.broadcasted_iota(jnp.int32, (4, 128), 0) * 128 + lax.broadcasted_iota(jnp.int32, (4, 128), 1)
    mine = ((lane >> 4) & 15) == b
    half_of = (lane >> 3) & 1
    task_of = (lane & 7) + 8 * (lane >> 8)
    row_of = jnp.full((4, 128), -1, jnp.int32)
    for k in range(NEAR + FARS):
        local = (near_row[k] if k < NEAR else far_row[k - NEAR]) - base
        row_of = jnp.where(mine & (task_of == k), 2 * local - (local & 1), row_of)
    place = jnp.where(row_of >= 0, row_of + 2 * half_of + 1, 0).astype(F32)
    plane[b] = jnp.concatenate([own_rhs, halves(self_term[...]), place, jnp.zeros((4, 128), F32)], axis=0)

    pl.semaphore_wait(barrier, 31 + len(both))

    pending = []

    def send(src, dst, send_sem, recv_sem, device):
        pltpu.make_async_remote_copy(
            src_ref=src, dst_ref=dst, send_sem=send_sem, recv_sem=recv_sem, device_id=device, device_id_type=MESH
        ).start()

    def whole_stage(ref, send_sem, recv_sem):
        return pltpu.make_async_remote_copy(
            src_ref=ref, dst_ref=ref, send_sem=send_sem, recv_sem=recv_sem, device_id=sibling, device_id_type=MESH
        )

    def arrived(ref, recv_sem):
        whole_stage(ref, recv_sem, recv_sem).wait_recv()

    def sending(ref, send_sem):
        pending.append(whole_stage(ref, send_sem, send_sem))

    def settle():
        while pending:
            pending.pop().wait_send()

    for i in ALONG:
        rank = RANKS[i]
        batch = (rank // 4 + 1) // 2
        send(own, along.at[rank], along_send.at[0], along_recv.at[batch], along_z(i))
        if batch == 2:
            send(own, along.at[rank + 4], along_send.at[0], along_recv.at[batch], along_z(i, 1 - c))
    sending(along.at[0:19], along_send.at[0])
    for j in PLANE:
        send(plane.at[b], plane.at[b], plane_send.at[0], plane_recv.at[0], (r, peer[j]))
    sending(plane.at[0:15], plane_send.at[0])

    task = lax.broadcasted_iota(jnp.int32, (32, 1), 0)
    half = task >> 4
    place_1 = jnp.full((32, 1), -1, jnp.int32)
    place_2 = jnp.full((32, 1), -1, jnp.int32)
    for k in range(NEAR + FARS):
        col = near_col[k] if k < NEAR else far_col[k - NEAR]
        other = ((col >> 5) & 1) ^ c
        d = ((col >> 6) - z + 16) & 15
        dev = (col >> 1) & 15
        cl = col & 1
        rank = jnp.where(d == 0, 0, jnp.where(d <= 8, 2 * d - 1, 32 - 2 * d))
        tile_of, low = rank >> 2, rank & 3

        row = low * 4 + cl
        in_first = other * 256 + dev * 16 + row
        in_middle = 512 + other * 512 + dev * 32 + (tile_of - 1) * 16 + row
        in_last = 1536 + dev * 32 + other * 16 + row
        p1 = jnp.where(tile_of == 0, in_first, jnp.where(tile_of == 3, in_last, in_middle))
        t = rank >> 1
        away = ((rank ^ t) & 1) ^ (x % 2)
        slot = away * 4 + (((dev >> 2) - y - 2 * (((x + away) & 3) >> 1) + 8) & 3)
        row = (dev & 3) * 4 + cl
        in_first = ((other * 8 + slot) * 2 + t) * 16 + row
        in_middle = 512 + ((other * 8 + slot) * 4 + t - 2) * 16 + row
        in_last = 1536 + ((slot * 2 + other) * 2 + t - 6) * 16 + row
        p2 = jnp.where(t < 2, in_first, jnp.where(t >= 6, in_last, in_middle))
        place_1 = jnp.where((task & 15) == k, p1 + 2 * half, place_1)
        place_2 = jnp.where((task & 15) == k, p2 + 2 * half, place_2)
    spot = lax.broadcasted_iota(jnp.int32, (32, 512), 1)

    def hots(place, start, size):
        return jnp.where(spot[:, :size] + start == place, 1.0, 0.0).astype(BF16)

    for it, place in ((0, place_1), (1, place_2)):
        for other in range(2):
            hot_first[it, other] = hots(place, 256 * other, 256)
            hot_middle[it, other] = hots(place, 512 + 512 * other, 512)
        hot_last[it] = hots(place, 1536, 512)

    rank_of = jnp.zeros((16, 1), jnp.int32)
    task16 = lax.broadcasted_iota(jnp.int32, (16, 1), 0)
    for k in range(FARS):
        rank_of = jnp.where(task16 == NEAR + k, far_rank[k], rank_of)
    lane192 = lax.broadcasted_iota(jnp.int32, (16, FARS * RANK), 1)
    keep = ((lane192 >> 5) + NEAR == task16) & ((lane192 & 31) < rank_of)

    own_tiles = [[first_1.at[0], middle_1.at[0], last_1], [first_2.at[0], middle_2.at[0], last_2]]
    other_tiles = [[first_1.at[1], middle_1.at[1]], [first_2.at[1], middle_2.at[1]]]

    def send_batch(it, batch):
        held = own_tiles[it][batch]
        if it == 0:
            for j in PLANE:
                send(held.at[b], held.at[b], gather_send.at[it, batch], gather_recv.at[it, batch], (r, peer[j]))
            sending(held.at[0:15], gather_send.at[it, batch])
        else:
            for slot in (2, 5, 7, 1, 3, 4, 6):
                ox, oy = OFFSETS[slot]
                to = (r, ((x - ox + 4) % 4) * 4 + (y - oy + 4) % 4)
                send(held.at[0], held.at[slot], gather_send.at[it, batch], gather_recv.at[it, batch], to)
            sending(held.at[0:7], gather_send.at[it, batch])

    def finish_batch(it, batch):
        held = own_tiles[it][batch]
        arrived(held.at[0 : 7 if it else 15], gather_recv.at[it, batch])
        if batch < 2:
            send(held, other_tiles[it][batch], core_send.at[it, batch], core_recv.at[it, batch], sibling)
            sending(held, core_send.at[it, batch])

    def picked(hot, source):
        return jnp.dot(hot, source.reshape(-1, 128), preferred_element_type=F32)

    def joined(value):
        return jnp.concatenate([value[:16], value[16:]], axis=1)

    def hold_terms(it, kind, value):
        terms[it, kind, b] = halves(value).astype(BF16)

    def send_terms(it, kind):
        for j in PLANE:
            part = terms.at[it, kind, b]
            send(part, part, terms_send.at[it, kind], terms_recv.at[it, kind], (r, peer[j]))
        sending(terms.at[it, kind, 0:15], terms_send.at[it, kind])

    def take_terms(it, kind, select):
        arrived(terms.at[it, kind, 0:15], terms_recv.at[it, kind])
        return jnp.dot(select, terms[it, kind].reshape(256, 128), preferred_element_type=F32)

    def near_terms(picks):
        source = joined(picks)
        result = jnp.zeros((16, 256), F32)
        for k in range(NEAR):
            one = jnp.where(task16 == k, source, 0.0).astype(BF16)
            result += lax.dot_general(one, near[k], (((1,), (1,)), ((), ())), preferred_element_type=F32)
        return result[:8]

    def far_terms(picks):
        source = joined(picks).astype(BF16)
        coeff = lax.dot_general(
            source, right[...].reshape(FARS * RANK, 256), (((1,), (1,)), ((), ())), preferred_element_type=F32
        )
        coeff = jnp.where(keep, coeff, 0.0).astype(BF16)
        return jnp.dot(coeff, left[...].reshape(FARS * RANK, 256), preferred_element_type=F32)[8:]

    def send_sums(stage, values):
        lanes = lax.broadcasted_iota(jnp.int32, (1, 128), 1)
        row = jnp.zeros((1, 128), F32)
        for n, value in enumerate(values):
            row = jnp.where(lanes == n, value, row)
        sums[stage, 0] = row
        for i in ALONG:
            slot = RANKS[i]
            far = int(slot > 8)
            send(sums.at[stage, 0], sums.at[stage, slot], sums_send.at[stage], sums_recv.at[stage, far], along_z(i))
            if far and stage == 2:
                there = sums.at[stage, slot + 7]
                send(sums.at[stage, 0], there, sums_send.at[stage], sums_recv.at[stage, 1], along_z(i, 1 - c))
        sending(sums.at[stage, 0 : 22 if stage == 2 else 15], sums_send.at[stage])

    def pair_sums(stage):
        arrived(sums.at[stage, 0:8], sums_recv.at[stage, 0])
        if stage < 2:
            arrived(sums.at[stage, 0:7], sums_recv.at[stage, 1])
        pair[stage, 0] = jnp.sum(sums[stage, 0 : 9 if stage == 2 else 16], axis=0)
        send(pair.at[stage, 0], pair.at[stage, 1], pair_send.at[stage], pair_recv.at[stage], sibling)
        sending(pair.at[stage, 0], pair_send.at[stage])

    def spread(value):
        return jnp.broadcast_to(value, (4, 128))

    def take_sums(stage, count):
        arrived(pair.at[stage, 1], pair_recv.at[stage])
        row = pair[stage, 0] + pair[stage, 1]
        if stage == 2:
            arrived(sums.at[stage, 0:14], sums_recv.at[stage, 1])
            row += jnp.sum(sums[stage, 9:23], axis=0)
        return [spread(row[:, n : n + 1]) if stage == 2 else row[:, n : n + 1] for n in range(count)]

    def along_batch(batch):
        start, stop, count = BOUNDS[batch]
        arrived(along.at[0:count], along_recv.at[batch])
        for e in range(start, stop):
            flat_along[4 * e : 4 * e + 4] = along[e]
        part = flat_along[4 * start : 4 * stop].astype(BF16)
        own_tiles[0][batch][b] = part if batch == 0 else part.reshape(2, 16, 128)
        send_batch(0, batch)

    along_batch(0)
    arrived(plane.at[0:15], plane_recv.at[0])
    index = jnp.zeros((4, 128), F32)
    for dev in range(16):
        flat_rhs[4 * dev : 4 * dev + 4] = plane[dev, 0:4]
        flat_self[4 * dev : 4 * dev + 4] = plane[dev, 4:8]
        index += plane[dev, 8:12]
    squares = flat_rhs[...] * flat_rhs[...]
    squares_here, diagonal_here = total(squares), total(squares * (flat_self[...] * 0.125))
    along_batch(1)
    along_batch(2)
    send_sums(0, [squares_here, diagonal_here])
    index = index.astype(jnp.int32)
    spots = lax.broadcasted_iota(jnp.int32, (64, 256), 0) + 1
    selects = [
        jnp.where(
            spots == jnp.concatenate([index[2 * kind : 2 * kind + 1], index[2 * kind + 1 : 2 * kind + 2]], axis=1),
            1.0, 0.0,
        ).astype(BF16)
        for kind in range(2)
    ]

    def operate(it, before):
        finish_batch(it, 0)
        picks = picked(hot_first[it, 0], own_tiles[it][0][...])
        arrived(other_tiles[it][0], core_recv.at[it, 0])
        picks += picked(hot_first[it, 1], other_tiles[it][0][...])
        if it == 0:
            for load in loads[7:]:
                load.wait()
        hold_terms(it, 0, near_terms(picks))
        pick[...] = picks
        finish_batch(it, 1)
        send_terms(it, 0)
        picks = pick[...] + picked(hot_middle[it, 0], own_tiles[it][1][...])
        arrived(other_tiles[it][1], core_recv.at[it, 1])
        picks += picked(hot_middle[it, 1], other_tiles[it][1][...])
        finish_batch(it, 2)
        picks += picked(hot_last[it], own_tiles[it][2][...])
        hold_terms(it, 1, far_terms(picks))
        send_terms(it, 1)
        pair_sums(it)
        known = before(take_terms(it, 0, selects[0]))
        return known, take_terms(it, 1, selects[1])

    def before_1(sums_near):
        beta_squared, diagonal = take_sums(0, 2)
        beta = jnp.sqrt(beta_squared)
        guess = 8.0 * (diagonal / beta_squared)
        inverse = 1.0 / beta
        first = flat_rhs[...] * inverse
        image = (flat_self[...] * flat_rhs[...] + sums_near) * inverse
        return beta, guess, inverse, first, image, image - guess * first, total(first * first)

    (beta, guess, inverse, first, image, shifted, g11_here), sums_far = operate(0, before_1)
    sums_far = sums_far * inverse
    image = image + sums_far
    shifted = shifted + sums_far

    tile[...] = shifted.astype(BF16).reshape(4, 16, 128)

    even, quarter = x % 2, (y + 2 * (x // 2)) % 4

    def tile_copy(t, core=0):
        rank = 2 * t + (1 - even if t % 2 else even)
        away = (rank + 1) // 2
        d = away * (2 * (rank % 2) - 1)
        batch = (t + 2) // 4
        held = own_tiles[1][batch].at[0]
        part = held.at[t] if batch == 0 else held.at[t - 2] if batch == 1 else held.at[core, t - 6]
        recv = tile_recv.at[t if batch == 0 else batch + 1]
        return pltpu.make_async_remote_copy(
            src_ref=tile.at[quarter], dst_ref=part, send_sem=tile_send.at[int(t > 0)], recv_sem=recv,
            device_id=along_z(-d, 1 - c if core else c), device_id_type=MESH,
        )

    for t, core in ((7, 0), (7, 1), (6, 0), (6, 1), (5, 0), (4, 0), (3, 0), (2, 0), (1, 0)):
        tile_copy(t, core).start()
    sending(first_2.at[0, 0:4, 0], tile_send.at[1])
    sending(middle_2.at[0, 0, 0:4], tile_send.at[1])
    sending(first_2.at[0, 0, 0:1], tile_send.at[1])

    @pl.when(even > 0)
    def _():
        tile_copy(0).start()

    @pl.when(even == 0)
    def _():
        first_2[0, 0, 0] = tile[quarter]


    @pl.when(even > 0)
    def _():
        tile_copy(0).wait_recv()

    tile_copy(1).wait_recv()
    send_batch(1, 0)
    send_sums(1, [g11_here, total(first * shifted), total(shifted * shifted)])
    arrived(middle_2.at[0, 0], tile_recv.at[2])
    send_batch(1, 1)
    arrived(last_2.at[0], tile_recv.at[3])
    send_batch(1, 2)

    def before_2(sums_near):
        g11, p1, p2 = take_sums(1, 3)
        h11 = guess * g11 + p1
        step = h11 - guess
        h21 = jnp.sqrt(jnp.maximum(p2 - 2.0 * step * p1 + step * step * g11, 0.0) + 1e-06)
        inverse = 1.0 / h21
        basis = (shifted - step * first) * inverse
        rest = (flat_self[...] * shifted + sums_near - step * image) * inverse - guess * basis
        radius = jnp.sqrt(h11 * h11 + h21 * h21)
        return g11, h11, h21, inverse, basis, rest, radius, total(first * basis), total(basis * basis)

    (g11, h11, h21, inverse, basis, rest, radius, g12_here, g22_here), sums_far = operate(1, before_2)
    rest = rest + sums_far * inverse
    send_sums(2, [total(first * rest), total(basis * rest), total(rest * rest), g12_here, g22_here])

    def mine_of(value):
        flat_along[0:64] = value
        two = flat_along[pl.ds(pl.multiple_of((b // 2) * 8, 8), 8), :]
        return jnp.where(b % 2 == 0, two[:4], two[4:])

    own_first, own_basis, own_rest = mine_of(first), mine_of(basis), mine_of(rest)
    turn = 1.0 / radius
    cosine, sine, sine_beta, cosine_beta = h11 * turn, h21 * turn, h21 * turn * beta, h11 * turn * beta
    turn, cosine, sine, sine_beta, cosine_beta = map(spread, (turn, cosine, sine, sine_beta, cosine_beta))
    guess, g11 = spread(guess), spread(g11)

    @pl.when(even > 0)
    def _():
        tile_copy(0).wait_send()

    settle()

    pair_sums(2)
    q1, q2, q3, g12, g22 = take_sums(2, 5)
    h12 = q1 + guess * g12
    h22 = q2 + guess * g22
    left_over = h22 - guess
    square = (
        q3 - 2.0 * h12 * q1 - 2.0 * left_over * q2
        + h12 * h12 * g11 + left_over * left_over * g22 + 2.0 * h12 * left_over * g12
    )
    square = jnp.maximum(square, 0.0) + 1e-06
    upper = cosine * h12 + sine * h22
    lower = cosine * h22 - sine * h12
    coef_two = -(lower / (lower * lower + square)) * sine_beta
    coef_one = (cosine_beta - upper * coef_two) * turn

    def wide(value):
        return jnp.concatenate([value[0:2], value[2:4]], axis=1)

    out[0] = wide(coef_one * own_first + coef_two * own_basis)
    out[1] = wide((own_rest - h12 * own_first - left_over * own_basis) * lax.rsqrt(square))

    settle()


def shards(rhs, self_term, near_blocks, near_row, near_col, far_left, far_right, far_row, far_col, far_rank):
    hbm = pl.BlockSpec(memory_space=pltpu.HBM)
    dma = pltpu.SemaphoreType.DMA
    out = pl.pallas_call(
        kernel,
        out_shape=pltpu.VMEM((2, *rhs.shape), F32),
        in_specs=[hbm] * 10,
        out_specs=pl.BlockSpec(memory_space=pltpu.VMEM),
        scratch_shapes=[
            *[pltpu.SMEM(a.shape, jnp.int32) for a in (near_row, near_col, far_row, far_col, far_rank)],
            pltpu.VMEM(rhs.shape, F32), pltpu.VMEM(rhs.shape, F32),
            pltpu.VMEM(near_blocks.shape, BF16), pltpu.VMEM(far_left.shape, BF16), pltpu.VMEM(far_right.shape, BF16),
            dma((10,)),
            pltpu.VMEM((4, 128), F32), pltpu.VMEM((20, 4, 128), F32), dma((1,)), dma((3,)),
            pltpu.VMEM((16, 16, 128), F32), dma((1,)), dma((1,)),
            pltpu.VMEM((2, 16, 16, 128), BF16), pltpu.VMEM((2, 16, 2, 16, 128), BF16), pltpu.VMEM((16, 2, 16, 128), BF16),
            pltpu.VMEM((2, 8, 2, 16, 128), BF16), pltpu.VMEM((2, 8, 4, 16, 128), BF16),
            pltpu.VMEM((8, 2, 2, 16, 128), BF16), dma((2, 3)), dma((2, 3)), dma((2, 2)), dma((2, 2)),
            pltpu.VMEM((2, 2, 16, 16, 128), BF16), dma((2, 2)), dma((2, 2)),
            pltpu.VMEM((4, 16, 128), BF16), dma((2,)), dma((4,)),
            pltpu.VMEM((3, 23, 1, 128), F32), dma((3,)), dma((3, 2)),
            pltpu.VMEM((3, 2, 1, 128), F32), dma((3,)), dma((3,)),
            pltpu.VMEM((2, 2, 32, 256), BF16), pltpu.VMEM((2, 2, 32, 512), BF16), pltpu.VMEM((2, 32, 512), BF16),
            pltpu.VMEM((64, 128), F32), pltpu.VMEM((64, 128), F32), pltpu.VMEM((80, 128), F32),
            pltpu.VMEM((32, 128), F32),
        ],
        compiler_params=pltpu.CompilerParams(
            collective_id=0, has_side_effects=True, vmem_limit_bytes=56 * 1024 * 1024
        ),
        name="gmres",
    )(near_row, near_col, far_row, far_col, far_rank, rhs, self_term, near_blocks, far_left, far_right)
    return out[0], out[1]


def solution(mesh):
    vec = P(("rows", "bal"), None)
    blocks = P(("rows", "bal"), None, None)
    ints = P(("rows", "bal"))
    in_specs = (vec, vec, blocks, ints, ints, blocks, blocks, ints, ints, ints)
    return jax.shard_map(shards, mesh=mesh, in_specs=in_specs, out_specs=(vec, vec), check_vma=False)
```
